128 devices in a mesh: dp: 64 (over z_hi, y, x, core), tensor: 2 (over z_lo).
Axes of the slice: x: 4, y: 4, z: 4 (z_hi: 2, z_lo: 2; z = z_hi * 2 + z_lo), core: 2. Of those that a mesh axis runs over, the one named last changes fastest.
Arguments:
- tokens: bfloat16 [64, 1024, 768], P('dp', 'tensor'), may hold values from -6 to 6
- segments: int32 [64, 1024], P('dp', 'tensor'), may hold values from 0 to 319, as said below
- cotangent: bfloat16 [64, 1024, 768], P('dp', 'tensor'), may hold values from -16 to 16
- w_qkv: bfloat16 [3, 768, 768], P(None, 'dp', 'tensor'), may hold values from -0.21875 to 0.21875
- b_qv: bfloat16 [2, 12, 64], P(None, 'tensor', 'dp'), may hold values from -3 to 3
- w_proj: bfloat16 [768, 768], P('tensor', 'dp'), may hold values from -0.875 to 0.875
- w_fc: bfloat16 [768, 3072], P('dp', 'tensor'), may hold values from -0.21875 to 0.21875
- b_fc: bfloat16 [48, 64], P('tensor', 'dp'), may hold values from -3 to 3
- w_out: bfloat16 [3072, 768], P('tensor', 'dp'), may hold values from -0.15625 to 0.15625
- ln_gains: float32 [2, 768], P(None, ('dp', 'tensor')), may hold values from 0.5 to 1.5
- ln_biases: float32 [2, 768], P(None, ('dp', 'tensor')), may hold values from -1.75 to 1.75
- out_biases: float32 [2, 768], P(None, ('dp', 'tensor')), may hold values from -1.75 to 1.75
Outputs:
- block_out: bfloat16 [64, 1024, 768], P('dp', 'tensor')
- d_tokens: bfloat16 [64, 1024, 768], P('dp', 'tensor')
- d_w_qkv: float32 [3, 768, 768], P(None, 'dp', 'tensor')
- d_b_qv: float32 [2, 12, 64], P(None, 'tensor', 'dp')
- d_w_proj: float32 [768, 768], P('tensor', 'dp')
- d_w_fc: float32 [768, 3072], P('dp', 'tensor')
- d_b_fc: float32 [48, 64], P('tensor', 'dp')
- d_w_out: float32 [3072, 768], P('tensor', 'dp')
- d_ln_gains: float32 [2, 768], P(None, ('dp', 'tensor'))
- d_ln_biases: float32 [2, 768], P(None, ('dp', 'tensor'))
- d_out_biases: float32 [2, 768], P(None, ('dp', 'tensor'))
The draws below stay inside these ranges and needn't reach their ends.
Inputs may be any that keep to these rules, and one draw needn't show every extreme that they name: `segments`: numbers never fall along a row and no two rows share one; the first token of row r has r * 5, its last r * 5 + 4; no document begins within 128 positions of a row's middle.
All inputs are finite; a program needn't handle non-finite values.
Results may differ from the reference program's by a relative error of at most 0.012.
Values may be sent and summed in bfloat16 or wider, within the bound.
No kernel may reach another device: no remote copies, remote signals or barrier semaphores. Data moves between devices by JAX's collectives and lax.ppermute only.
A program may use at most 128 MiB of HBM per device.

```python
import jax
import jax.numpy as jnp
from jax import lax

D = 768
H = 12
HD = 64
FF = 3072
LEN = 1024
ROWS = 1
CUTS = 4
NROWS = 64
N_DP = 64


def draw_segments(key, part):
    key = jax.random.fold_in(key, 7)
    cut_points = jax.random.randint(key, (NROWS, CUTS), 1, LEN - LEN // 4, dtype=jnp.int32)
    lower_edge = LEN // 2 - LEN // 8
    cut_points = jnp.where(cut_points >= lower_edge, cut_points + LEN // 4, cut_points)
    places = jnp.arange(LEN, dtype=jnp.int32)
    passed = (cut_points[:, None, :] <= places[None, :, None]).astype(jnp.int32)
    numbers = jnp.sum(passed, axis=2).astype(jnp.int32)
    offsets = (jnp.arange(NROWS, dtype=jnp.int32) * (CUTS + 1)).astype(jnp.int32)
    return (numbers + offsets[:, None]).astype(jnp.int32)


def strengthened(result, key, source, target, shards_of, factor):
    owner, partner = [(jnp.arange(result.shape[position]) // (result.shape[position] // shards_of)).reshape([-1 if axis == position else 1 for axis in range(result.ndim)]) for position in (source, target)]
    chosen = jax.random.permutation(key, shards_of)[partner]
    strong = (owner == chosen) | (owner == (partner + shards_of // 2) % shards_of)
    return jnp.where(strong, factor * result, result)


def levels(rng, extent, split, least, top_value):
    def one(axis_at, shards_of):
        draws = jax.random.uniform(jax.random.fold_in(jax.random.fold_in(rng, 6), axis_at), (shards_of,), jnp.float32, least / len(split), top_value / len(split))
        return jnp.repeat(jnp.exp(draws), extent[axis_at] // shards_of).reshape((-1,) + (1,) * (len(extent) - axis_at - 1))

    level = one(*split[0])
    for cut in split[1:]:
        level = level * one(*cut)
    return level


def bell_draw(stream_key, dims, width, reach, split=(), kind=jnp.bfloat16):
    loudness = levels(stream_key, dims, split, -0.22, 0.18) if split else 1.0
    entries = jax.random.normal(stream_key, dims, jnp.float32) * width * loudness
    return jnp.minimum(jnp.maximum(entries, -reach), reach).astype(kind)


def noise_with(stream_key, extent, spread, limit, pieces, heavy, kind=jnp.bfloat16):
    result = spread * jax.random.normal(stream_key, extent, jnp.float32)
    if pieces:
        result = result * levels(stream_key, extent, pieces, -0.22, 0.18)
    return jnp.clip(strengthened(result, jax.random.fold_in(stream_key, 3), *heavy), -limit, limit).astype(kind)


def setup_inputs(seed: int = 0) -> dict:
    keys = jax.random.split(jax.random.key(seed), 13)
    return {
        "tokens": bell_draw(keys[0], (NROWS, LEN, D), 1.0, 6.0, ((0, 64), (1, 2))),
        "segments": draw_segments(jax.random.fold_in(keys[12], 71), 0),
        "cotangent": noise_with(keys[2], (NROWS, LEN, D), 1.0, 16.0, ((0, 64), (1, 2)), (0, 2, 64, 4.0)),
        "w_qkv": bell_draw(keys[3], (3, D, D), D ** -0.5, 0.21875, ((1, 64), (2, 2))),
        "b_qv": bell_draw(keys[4], (2, H, HD), 0.5, 3.0, ((1, 2), (2, 64))),
        "w_proj": bell_draw(keys[5], (D, D), (D // 16) ** -0.5, 0.875, ((0, 2), (1, 64))),
        "w_fc": bell_draw(keys[6], (D, FF), D ** -0.5, 0.21875, ((0, 64), (1, 2))),
        "b_fc": bell_draw(keys[7], (FF // HD, HD), 0.5, 3.0, ((0, 2), (1, 64))),
        "w_out": bell_draw(keys[8], (FF, D), (FF // 2) ** -0.5, 0.15625, ((0, 2), (1, 64))),
        "ln_gains": jnp.clip(1.0 + 0.1 * jax.random.normal(keys[9], (2, D), jnp.float32), 0.5, 1.5),
        "ln_biases": bell_draw(keys[10], (2, D), 0.3, 1.75, ((1, 128),), jnp.float32),
        "out_biases": bell_draw(keys[11], (2, D), 0.3, 1.75, ((1, 128),), jnp.float32),
    }


@jax.custom_vjp
def low(v):
    return lax.optimization_barrier(v.astype(jnp.bfloat16)).astype(jnp.float32)

@jax.custom_vjp
def low_back(v):
    return v

def low_keep(v):
    return (low(v), None)

def low_pass(kept, grad):
    return (grad,)

def back_keep(v):
    return (v, None)

def back_low(kept, grad):
    return (low(grad),)
low.defvjp(low_keep, low_pass)
low_back.defvjp(back_keep, back_low)

def norm_rows(values, norm_gain, norm_shift):
    average = lax.optimization_barrier(jnp.mean(values, axis=-1, keepdims=True))
    centred = values - average
    variance = lax.optimization_barrier(jnp.mean(centred * centred, axis=-1, keepdims=True))
    return centred * lax.rsqrt(variance + 1e-05) * norm_gain + norm_shift

def gelu_tanh(inputs):
    return 0.5 * inputs * (1.0 + jnp.tanh(0.7978845608028654 * (inputs + 0.044715 * inputs * inputs * inputs)))

def attend_row(bundle):
    queries, key_rows, values, segment_ids = bundle
    scores = low_back(0.125 * jnp.einsum('qhd,khd->hqk', queries, key_rows, precision=lax.Precision.HIGHEST))
    places = jnp.arange(segment_ids.shape[0], dtype=jnp.int32)
    allowed = (segment_ids[:, None] == segment_ids[None, :]) & (places[:, None] >= places[None, :])
    scores = jnp.where(allowed[None], scores, -1e+30)
    attn_probs = jax.nn.softmax(scores, axis=-1)
    return jnp.einsum('hqk,khd->qhd', low(attn_probs), values, precision=lax.Precision.HIGHEST)

def forward(inputs, segment_ids, w_qkv, b_qv, w_proj, w_fc, b_fc, w_out, ln_gains, ln_biases, out_biases):
    highest = lax.Precision.HIGHEST
    row_count, length, model_width = inputs.shape
    flat = inputs.reshape(row_count * length, model_width)
    first = low(norm_rows(flat, ln_gains[0], ln_biases[0]))
    queries = low(low_back(jnp.dot(first, w_qkv[0], precision=highest) + b_qv[0].reshape(-1)))
    key_rows = low(low_back(jnp.dot(first, w_qkv[1], precision=highest)))
    values = low(low_back(jnp.dot(first, w_qkv[2], precision=highest) + b_qv[1].reshape(-1)))
    head_shape = (row_count, length, H, HD)
    mixed = lax.map(jax.checkpoint(attend_row), (queries.reshape(head_shape), key_rows.reshape(head_shape), values.reshape(head_shape), segment_ids))
    heads_out = low(low_back(mixed.reshape(row_count * length, model_width)))
    branch_one = low_back(jnp.dot(heads_out, w_proj, precision=highest) + out_biases[0])
    midway_tokens = flat + branch_one
    second = low(norm_rows(midway_tokens, ln_gains[1], ln_biases[1]))
    hidden_pre = low_back(jnp.dot(second, w_fc, precision=highest) + b_fc.reshape(-1))
    activation = low(gelu_tanh(hidden_pre))
    branch_two = low_back(jnp.dot(activation, w_out, precision=highest) + out_biases[1])
    return (midway_tokens + branch_two).reshape(row_count, length, model_width)

def reference(tokens, segments, cotangent, w_qkv, b_qv, w_proj, w_fc, b_fc, w_out, ln_gains, ln_biases, out_biases):
    params = tuple((p.astype(jnp.float32) for p in (w_qkv, b_qv, w_proj, w_fc, b_fc, w_out, ln_gains, ln_biases, out_biases)))
    token_groups = tokens.reshape(N_DP, ROWS, LEN, D)
    segment_groups = segments.reshape(N_DP, ROWS, LEN)
    grad_groups = cotangent.reshape(N_DP, ROWS, LEN, D)

    def one_group(running, bundle):
        group_tokens, group_segments, group_grad = bundle

        def local_forward(inputs, *weights):
            return forward(inputs, group_segments, *weights)
        outcome, pullback = jax.vjp(local_forward, group_tokens.astype(jnp.float32), *params)
        grads = pullback(group_grad.astype(jnp.float32))
        running = tuple((a + b for a, b in zip(running, grads[1:])))
        return (running, (outcome.astype(jnp.bfloat16), grads[0].astype(jnp.bfloat16)))
    zeros = tuple((jnp.zeros_like(p) for p in params))
    totals, (outcomes, input_grads) = lax.scan(one_group, zeros, (token_groups, segment_groups, grad_groups))
    block_out = outcomes.reshape(NROWS, LEN, D)
    d_tokens = input_grads.reshape(NROWS, LEN, D)
    return (block_out, d_tokens, totals[0], totals[1], totals[2], totals[3], totals[4], totals[5], totals[6], totals[7], totals[8])
```

```python
import jax
import jax.numpy as jnp
from jax import lax
from jax.experimental import pallas as pl
from jax.experimental.pallas import tpu as pltpu
from jax.sharding import Mesh, PartitionSpec as P

AXES = ("zh", "y", "x", "core", "zl")
DP = ("zh", "y", "x", "core")
Z = ("zh", "zl")
HALF = 512
WIDTH = 768
FF = 3072
BF = jnp.bfloat16
F32 = jnp.float32
VMEM = 60 * 1024 * 1024


def swap(value, axis, bit):
    count = 2 if axis == "core" else 4
    return lax.ppermute(value, axis, [(i, i ^ bit) for i in range(count)])


def dot(a, b, ca, cb):
    return lax.dot_general(a, b, (((ca,), (cb,)), ((), ())), preferred_element_type=F32)


def together(*values):
    return lax.optimization_barrier(values)


def after(value, *earlier):
    return lax.optimization_barrier((value, earlier))[0]


def combine(inputs, outputs, plan):
    def kernel(*refs):
        sources, results = refs[: len(inputs)], refs[len(inputs) :]
        for out, r, c, rows, cols, terms in plan:
            read = [sources[i][a : a + rows, b : b + cols] for i, a, b in terms]
            total = read[0]
            if len(read) > 1:
                total = total.astype(F32)
                for term in read[1:]:
                    total = total + term.astype(F32)
            results[out][r : r + rows, c : c + cols] = total.astype(results[out].dtype)

    moved = sum(2 * v.size for v in inputs) + sum(2 * r * c for r, c in outputs)
    return pl.pallas_call(
        kernel,
        out_shape=[jax.ShapeDtypeStruct(shape, BF) for shape in outputs],
        compiler_params=pltpu.CompilerParams(vmem_limit_bytes=VMEM),
        cost_estimate=pl.CostEstimate(flops=0, bytes_accessed=moved, transcendentals=0),
    )(*inputs)


def place(inputs, outputs, plan):
    def kernel(*refs):
        sources = refs[: len(inputs)]
        results = refs[len(inputs) : len(inputs) + len(outputs)]
        sems = refs[-1]
        copies = [
            pltpu.make_async_copy(
                sources[i].at[a : a + rows, b : b + cols],
                results[out].at[r : r + rows, c : c + cols],
                sems.at[n],
            )
            for n, (out, r, c, rows, cols, (i, a, b)) in enumerate(plan)
        ]
        for copy in copies:
            copy.start()
        for copy in copies:
            copy.wait()

    return pl.pallas_call(
        kernel,
        out_shape=[jax.ShapeDtypeStruct(shape, BF) for shape in outputs],
        in_specs=[pl.BlockSpec(memory_space=pl.ANY)] * len(inputs),
        scratch_shapes=[pltpu.SemaphoreType.DMA((len(plan),))],
        compiler_params=pltpu.CompilerParams(vmem_limit_bytes=VMEM),
        cost_estimate=pl.CostEstimate(
            flops=0, bytes_accessed=sum(4 * r * c for r, c in outputs), transcendentals=0
        ),
    )(*inputs)


def others(part, axis):
    return [swap(part, axis, k) for k in (1, 2, 3)]


def join_z(pieces, widths):
    plan, at = [], 0
    for width in widths:
        for bit in range(4):
            plan.append((0, bit // 2 * 48, 2 * at + bit % 2 * width, 48, width, (bit, 0, at)))
        at += width
    return place(pieces, [(96, 2 * at)], plan)[0]


def join_y(pieces):
    width = pieces[0].shape[1]
    return place(pieces, [(192, width)], [(0, 48 * k, 0, 48, width, (k, 0, 0)) for k in range(4)])[0]


def with_core(pieces):
    return [swap(piece, "core", 1) for piece in pieces]


def assemble_y(pieces, cuts):
    plan, pairs = [], list(zip((0,) + cuts[:-1], cuts))
    for out, (a, b) in enumerate(pairs):
        plan += [(out, 96 * i, 0, 96, b - a, (i, 0, a)) for i in range(8)]
    return place(pieces, [(WIDTH, b - a) for a, b in pairs], plan)


def assemble_z(pieces):
    width = pieces[0].shape[1]
    plan = []
    for i in range(8):
        core, bit = i // 4, i % 4
        for k in range(4):
            row = core * 384 + k * 96 + bit // 2 * 48
            plan.append((0, row, bit % 2 * width, 48, width, (i, 48 * k, 0)))
    return place(pieces, [(WIDTH, 2 * width)], plan)[0]


def send_core(parts):
    return [swap(sent, "core", 1) for _, sent in parts]


def to_y_blocks(parts, came):
    plan, at, count = [], 0, len(parts)
    for i, (own, _) in enumerate(parts):
        width = own.shape[1]
        for k in range(4):
            plan.append((k, 0, at, 96, width, [(i, 96 * k, 0), (count + i, 96 * k, 0)]))
        at += width
    return combine([own for own, _ in parts] + came, [(96, at)] * 4, plan)


def to_z_blocks(parts, came):
    plan, at, count = [], 0, len(parts)
    for i, (own, _) in enumerate(parts):
        width = own.shape[1] // 2
        for bit in range(4):
            for k in range(4):
                row, col = 96 * k + bit // 2 * 48, bit % 2 * width
                plan.append((bit, 48 * k, at, 48, width, [(i, row, col), (count + i, row, col)]))
        at += width
    return combine([own for own, _ in parts] + came, [(192, at)] * 4, plan)


def send(blocks, axis):
    return [blocks[0]] + [swap(blocks[k], axis, k) for k in (1, 2, 3)]


def y_then_z_blocks(groups, widths):
    plan, at = [], 0
    for g, group_widths in enumerate(widths):
        col = 0
        for width in group_widths:
            for bit in range(4):
                shared = groups[g][0].shape[1] == width
                row, c = bit // 2 * 48, col + (0 if shared else bit % 2 * width)
                plan.append((bit, 0, at, 48, width, [(4 * g + i, row, c) for i in range(4)]))
            col += 2 * width
            at += width
    return combine(sum(groups, []), [(48, at)] * 4, plan)


def z_then_y_blocks(groups):
    plan, at = [], 0
    for g, group in enumerate(groups):
        width = group[0].shape[1]
        for k in range(4):
            plan.append((k, 0, at, 48, width, [(4 * g + i, 48 * k, 0) for i in range(4)]))
        at += width
    return combine(sum(groups, []), [(48, at)] * 4, plan)


def total_of(groups):
    plan, at = [], 0
    for g, group in enumerate(groups):
        width = group[0].shape[1]
        plan.append((0, 0, at, 48, width, [(4 * g + i, 0, 0) for i in range(4)]))
        at += width
    return combine(sum(groups, []), [(48, at)], plan)[0]


def finish_x(low):
    total = low[:12].astype(F32)
    for k in (1, 2, 3):
        total = total + swap(low[12 * k : 12 * k + 12], "x", k).astype(F32)
    return total


def halves(a, b):
    return dot(a[:, :384], b, 0, 0).astype(BF), dot(a[:, 384:], b, 0, 0).astype(BF)


def lanes_of(head, value):
    lane = lax.broadcasted_iota(jnp.int32, value.shape, 1)
    return jnp.where((lane >= 64) == (head == 1), value, jnp.zeros_like(value))


def attend_kernel(q_ref, k_ref, v_ref, segq_ref, segk_ref, out_ref, p_ref, bias_ref):
    @pl.when(pl.program_id(0) == 0)
    def _():
        place_k = lax.broadcasted_iota(jnp.int32, (2 * HALF, HALF), 0)
        place_q = lax.broadcasted_iota(jnp.int32, (2 * HALF, HALF), 1) + HALF
        allowed = (segk_ref[...] == segq_ref[...]) & (place_k <= place_q)
        bias_ref[...] = jnp.where(allowed, 0.0, -1e30)

    for block in range(2):
        keys = HALF + 256 * (block + 1)
        rows = slice(256 * block, 256 * (block + 1))
        q = q_ref[rows, :] * 0.125
        k = k_ref[:keys, :]
        mixed = []
        for head in range(2):
            s = dot(k, lanes_of(head, q), 1, 1) + bias_ref[:keys, rows]
            e = jnp.exp(s - jnp.max(s, axis=0, keepdims=True))
            p = (e * (1.0 / jnp.sum(e, axis=0, keepdims=True))).astype(BF)
            p_ref[head, :keys, rows] = p
            mixed.append(dot(v_ref[:keys, :], p, 0, 0))
        feature = lax.broadcasted_iota(jnp.int32, mixed[0].shape, 0)
        out_ref[rows, :] = jnp.where(feature < 64, mixed[0], mixed[1]).T.astype(BF)


def attend(qkv, seg_q, seg_k, first, filled=None):
    whole = lambda shape: pl.BlockSpec(shape, lambda i: (0, 0))
    kept = [] if filled is None else [filled]

    def kernel(*refs):
        attend_kernel(*refs[:5], *refs[5 + len(kept) :])

    return pl.pallas_call(
        kernel,
        grid=(3,),
        in_specs=[
            pl.BlockSpec((HALF, 128), lambda i: (1, i + first)),
            pl.BlockSpec((2 * HALF, 128), lambda i: (0, i + first + 6)),
            pl.BlockSpec((2 * HALF, 128), lambda i: (0, i + first + 12)),
            whole((1, HALF)),
            whole((2 * HALF, 1)),
        ]
        + [pl.BlockSpec(memory_space=pl.ANY)] * len(kept),
        input_output_aliases={5: 0} if kept else {},
        out_specs=[
            pl.BlockSpec((HALF, 128), lambda i: (0, i + first)),
            pl.BlockSpec((2, 2 * HALF, HALF), lambda i: (i, 0, 0)),
        ],
        out_shape=[
            jax.ShapeDtypeStruct((HALF, WIDTH), BF),
            jax.ShapeDtypeStruct((6, 2 * HALF, HALF), BF),
        ],
        scratch_shapes=[pltpu.VMEM((2 * HALF, HALF), F32)],
        compiler_params=pltpu.CompilerParams(vmem_limit_bytes=VMEM),
        cost_estimate=pl.CostEstimate(
            flops=6 * HALF * HALF * 2 * 64 * 4, bytes_accessed=9_000_000, transcendentals=3_000_000
        ),
    )(qkv, qkv, qkv, seg_q, seg_k, *kept)


def attend_back_kernel(q_ref, k_ref, v_ref, p_ref, g_ref, dq_ref, dk_ref, dv_ref):
    dk_sum, dv_sum = None, None
    for block in range(2):
        keys = HALF + 256 * (block + 1)
        rows = slice(256 * block, 256 * (block + 1))
        q = q_ref[rows, :] * 0.125
        g = g_ref[rows, :]
        k = k_ref[:keys, :]
        v = v_ref[:keys, :]
        dq, dk, dv = [], [], []
        for head in range(2):
            p = p_ref[head, :keys, rows]
            dp = dot(v, lanes_of(head, g), 1, 1)
            wide = p.astype(F32)
            inner = jnp.sum(wide * dp, axis=0, keepdims=True)
            ds = (wide * (dp - inner)).astype(BF)
            dv.append(dot(p, g, 1, 0))
            dk.append(dot(ds, q, 1, 0))
            dq.append(dot(k, ds, 0, 0))
        feature = lax.broadcasted_iota(jnp.int32, dq[0].shape, 0)
        dq_ref[rows, :] = (jnp.where(feature < 64, dq[0], dq[1]).T * 0.125).astype(BF)
        lane = lax.broadcasted_iota(jnp.int32, dk[0].shape, 1)
        dk = jnp.where(lane < 64, dk[0], dk[1])
        dv = jnp.where(lane < 64, dv[0], dv[1])
        if block == 0:
            dk_sum, dv_sum = dk, dv
        else:
            seen = HALF + 256
            dk_ref[:seen, :] = (dk_sum + dk[:seen]).astype(BF)
            dv_ref[:seen, :] = (dv_sum + dv[:seen]).astype(BF)
            dk_ref[seen:, :] = dk[seen:].astype(BF)
            dv_ref[seen:, :] = dv[seen:].astype(BF)


def attend_back(qkv, p, grad, first, filled=()):
    narrow = pl.BlockSpec((HALF, 128), lambda i: (0, i + first))
    tall = pl.BlockSpec((2 * HALF, 128), lambda i: (0, i + first))

    def kernel(*refs):
        attend_back_kernel(*refs[:5], *refs[5 + len(filled) :])

    return pl.pallas_call(
        kernel,
        grid=(3,),
        in_specs=[
            pl.BlockSpec((HALF, 128), lambda i: (1, i + first)),
            pl.BlockSpec((2 * HALF, 128), lambda i: (0, i + first + 6)),
            pl.BlockSpec((2 * HALF, 128), lambda i: (0, i + first + 12)),
            pl.BlockSpec((2, 2 * HALF, HALF), lambda i: (i, 0, 0)),
            pl.BlockSpec((HALF, 128), lambda i: (0, i + first)),
        ]
        + [pl.BlockSpec(memory_space=pl.ANY)] * len(filled),
        input_output_aliases={5 + n: n for n in range(len(filled))},
        out_specs=[narrow, tall, tall],
        out_shape=[
            jax.ShapeDtypeStruct((HALF, WIDTH), BF),
            jax.ShapeDtypeStruct((2 * HALF, WIDTH), BF),
            jax.ShapeDtypeStruct((2 * HALF, WIDTH), BF),
        ],
        compiler_params=pltpu.CompilerParams(vmem_limit_bytes=VMEM),
        cost_estimate=pl.CostEstimate(
            flops=6 * HALF * HALF * 2 * 64 * 8, bytes_accessed=10_000_000, transcendentals=0
        ),
    )(qkv, qkv, qkv, p, grad, *filled)


def standard(values):
    centred = values - jnp.mean(values, axis=-1, keepdims=True)
    variance = jnp.mean(centred * centred, axis=-1, keepdims=True)
    inverse = lax.rsqrt(variance + 1e-05)
    return centred * inverse, inverse


def norm_back(gradient, normed, inverse, gain):
    scaled = gradient * gain
    first = jnp.mean(scaled, axis=-1, keepdims=True)
    second = jnp.mean(scaled * normed, axis=-1, keepdims=True)
    return (
        inverse * (scaled - first - normed * second),
        jnp.sum(gradient * normed, axis=0),
        jnp.sum(gradient, axis=0),
    )


def gelu_both(u):
    inner = 0.7978845608028654 * (u + 0.044715 * u * u * u)
    t = jnp.tanh(inner)
    slope = 0.7978845608028654 * (1.0 + 3.0 * 0.044715 * u * u)
    return 0.5 * u * (1.0 + t), 0.5 * (1.0 + t) + 0.5 * u * (1.0 - t * t) * slope


def feature_order():
    place = jnp.arange(WIDTH, dtype=jnp.int32)
    row, owner = place % 12, place // 12
    zh = lax.axis_index("zh") ^ (owner // 4 % 2)
    y = lax.axis_index("y") ^ (owner // 8 % 4)
    x = lax.axis_index("x") ^ (owner % 4)
    core = lax.axis_index("core") ^ (owner // 32)
    return ((zh * 4 + y) * 4 + x) * 2 + core, row


def body(
    tokens, segments, cotangent, w_qkv, b_qv, w_proj, w_fc, b_fc, w_out, ln_gains, ln_biases, out_biases
):
    first_half = lax.axis_index("zl") == 0
    before = lambda v: lax.ppermute(v, "zl", [(0, 1)])
    vectors = jnp.concatenate([ln_gains, ln_biases, out_biases], 0)
    high = lax.reduce_precision(vectors, 8, 7)
    middle = lax.reduce_precision(vectors - high, 8, 7)
    terms = jnp.concatenate([high, middle, vectors - high - middle], 0).T
    empty = jnp.zeros_like(terms)
    terms = jnp.where(
        first_half, jnp.concatenate([terms, empty], 0), jnp.concatenate([empty, terms], 0)
    ).astype(BF)
    extra = jnp.concatenate(
        [terms, b_qv.reshape(12, 1), b_fc.reshape(2, 12).T, jnp.zeros((12, 107), BF)], 1
    )
    weights = jnp.concatenate([*w_qkv, extra, w_fc, w_out.T, w_proj.T], 1)
    pieces = [weights] + others(weights, "x")
    one, two, three = [
        jnp.concatenate([v[:, a:b] for v in pieces], 0)
        for a, b in ((0, 1280), (1280, 2816), (2816, 4736))
    ]
    one = join_z([one] + others(one, Z), (384, 384, 384, 128))
    early, late, own_segments, cot = after(
        (tokens[0, :256], tokens[0, 256:], segments[0], cotangent[0]), one
    )

    owner, row = feature_order()
    turn = (
        jnp.arange(WIDTH, dtype=jnp.int32)[:, None] == (owner * 12 + row)[None, :]
    ).astype(BF)
    index = lambda n: jnp.arange(n, dtype=jnp.int32)
    of_owner = (owner[:, None] == index(64)[None, :]).astype(BF)
    of_row = (row[:, None] == index(72)[None, :] % 12).astype(F32)
    column = (index(128)[None, :] - index(72)[:, None] // 12).astype(F32)
    turn, of_owner, of_row, column = together(turn, of_owner, of_row, column)

    own_core, prev_a, prev_segments, prev_b, pieces, ones = together(
        with_core([one]),
        before(early),
        before(own_segments),
        before(late),
        [three] + others(three, Z),
        others(one, "y"),
    )
    prev_segments = jnp.where(first_half, -1, prev_segments)
    three = join_z(pieces, (1536, 384))
    whole_row = jnp.concatenate([prev_a, prev_b, tokens[0]], 0)
    stream = dot(whole_row, turn, 1, 0).astype(BF).astype(F32)
    grad_low = dot(cot, turn, 1, 0).astype(BF)
    xhat1, inv1 = standard(stream)
    ones_core, pieces, xhat1, inv1, grad_low = together(
        with_core(ones), [two] + others(two, "y"), xhat1, inv1, grad_low
    )
    two = join_y(pieces)
    one = [one] + ones + own_core + ones_core
    two, three, one = together(two, three, one)
    twos, threes = others(two, Z), others(three, "y")
    two_core, three_core = with_core([two]), with_core([three])
    one, small = assemble_y(one, (2304, 2560))
    w_q, w_k, w_v = one[:, :768], one[:, 768:1536], one[:, 1536:]

    terms = ((index(128)[None, :] % 6 == index(8)[:, None]) & (index(128)[None, :] < 18)).astype(BF)
    vectors = dot(terms, small[:, :128], 1, 1) + dot(terms, small[:, 128:], 1, 1)
    gains, shifts, biases = vectors[0:2], vectors[2:4], vectors[4:6]

    def entries(part):
        spread = dot(part, (column[:36] == 18).astype(BF), 1, 1) * of_row[:, :36]
        return dot(spread.astype(BF), of_owner, 0, 0)

    own_bias, other_bias = entries(small[:, :128]), entries(small[:, 128:])
    rows_of = lambda a, b: jnp.concatenate([own_bias[a:b], other_bias[a:b]], 0).reshape(-1)
    bias_q, bias_v, bias_f = rows_of(0, 6), rows_of(6, 12), rows_of(12, 36)

    a1 = (xhat1 * gains[0] + shifts[0]).astype(BF)
    stream, xhat1, inv1 = stream[HALF:], xhat1[HALF:], inv1[HALF:]
    zeros = jnp.zeros((WIDTH,), F32)
    qkv_bias = jnp.concatenate([bias_q, zeros, bias_v])
    qkv = (dot(a1, one, 1, 0) + qkv_bias).astype(BF)
    seg_k = jnp.concatenate([prev_segments, segments[0]], 0)[:, None]
    attn, probs_a = attend(qkv, segments, seg_k, 0)
    attn, probs_b = attend(qkv, segments, seg_k, 3, attn)
    attn, twos, threes, two_core, three_core = together(attn, twos, threes, two_core, three_core)
    two = [two] + twos + two_core + with_core(twos)
    three = [three] + threes + three_core + with_core(threes)
    w_o, w_p = assemble_y(three, (3072, 3840))
    w_f = assemble_z(two)

    r1 = stream + dot(attn, w_p, 1, 1) + biases[0]
    xhat2, inv2 = standard(r1)
    a2 = (xhat2 * gains[1] + shifts[1]).astype(BF)
    act, slope = gelu_both(dot(a2, w_f, 1, 0) + bias_f)
    act = act.astype(BF)
    parts_o = [halves(grad_low, act)]
    came_o = send_core(parts_o)
    grad_next, parts_o = lax.optimization_barrier((grad_low, parts_o))
    out = (r1 + dot(act, w_o, 1, 1) + biases[1]).astype(BF)
    block_out = dot(after(out), turn, 1, 1).astype(BF)

    grad = grad_low.astype(F32)
    d_bias_two = jnp.sum(grad, axis=0)
    du = (dot(grad_next, w_o, 1, 0) * slope).astype(BF)
    d_bias_f = jnp.sum(du.astype(F32), axis=0)
    du, came_o = lax.optimization_barrier((du, came_o))
    blocks_o = send(to_y_blocks(parts_o, came_o), "y")
    parts_f = [halves(a2, du)]
    came_f = send_core(parts_f)
    du, parts_f = lax.optimization_barrier((du, parts_f))
    da2 = after(dot(du, w_f, 1, 1))
    dv2, d_gain_two, d_shift_two = norm_back(da2, xhat2, inv2, gains[1])
    dr1 = grad + dv2
    g1 = dr1.astype(BF)
    d_bias_one = jnp.sum(g1.astype(F32), axis=0)
    parts_p = [halves(g1, attn)]
    came_p = send_core(parts_p)
    dattn = dot(g1, w_p, 1, 0).astype(BF)
    dattn, blocks_o, came_f, came_p = lax.optimization_barrier((dattn, blocks_o, came_f, came_p))
    blocks_f = to_y_blocks(parts_f + parts_p, came_f + came_p)
    dattn, blocks_f = lax.optimization_barrier((dattn, blocks_f))
    blocks_f = send(blocks_f, "y")
    filled = attend_back(qkv, probs_a, dattn, 0)
    dq, dk, dv = attend_back(qkv, probs_b, dattn, 3, tuple(filled))
    dq, dk, dv, blocks_f = together(dq, dk, dv, blocks_f)
    da1_prev = (dot(dk[:HALF], w_k, 1, 1) + dot(dv[:HALF], w_v, 1, 1)).astype(BF)
    blocks_u = y_then_z_blocks([blocks_o, blocks_f], [(1536,), (1536, 384)])
    da1_prev, blocks_u, dq, dk, dv = together(da1_prev, blocks_u, dq, dk, dv)
    da1_sent = lax.ppermute(da1_prev, "zl", [(1, 0)])
    blocks_u = send(blocks_u, Z)
    sent = [dot(u[:, 384:], v, 0, 0).astype(BF) for u, v in ((a1[HALF:], dq), (a1, dk), (a1, dv))]
    dq, dk, dv, sent = together(dq, dk, dv, sent)
    came = [swap(v, "core", 1) for v in sent]
    parts = [
        (dot(u[:, :384], v, 0, 0).astype(BF), None) for u, v in ((a1[HALF:], dq), (a1, dk), (a1, dv))
    ]
    parts, came = together(parts, came)
    blocks = to_y_blocks(parts, came)
    dq, dk, dv, blocks = together(dq, dk, dv, blocks)
    blocks = send(blocks, "y")
    da1 = dot(dq, w_q, 1, 1) + dot(dk[HALF:], w_k, 1, 1) + dot(dv[HALF:], w_v, 1, 1)
    da1, da1_sent = together(da1, da1_sent)
    da1 = da1 + da1_sent.astype(F32)
    dv1, d_gain_one, d_shift_one = norm_back(da1, xhat1, inv1, gains[0])
    d_tokens = dot(after((dr1 + dv1).astype(BF)), turn, 1, 1).astype(BF)

    d_bias_q = jnp.sum(dq.astype(F32), axis=0).reshape(2, 6, 64)
    d_bias_v = jnp.sum(dv.astype(F32), axis=0).reshape(2, 6, 64)
    d_bias_f = d_bias_f.reshape(2, 24, 64)
    per_head = jnp.concatenate([d_bias_q, d_bias_v, d_bias_f], 1)
    per_head = jnp.where(first_half, per_head, per_head[::-1]).reshape(72, 64).astype(BF)
    per_head = (dot(of_owner, per_head, 1, 1) * of_row).astype(BF)
    per_feature = jnp.stack(
        [d_gain_one, d_gain_two, d_shift_one, d_shift_two, d_bias_one, d_bias_two]
    ).astype(BF)
    extra = dot(per_feature, jnp.eye(6, 128, dtype=BF), 0, 0)
    extra = (extra + dot(per_head, (column == 6).astype(BF), 1, 0)).astype(BF)
    came = swap(extra[384:], "core", 1)
    extra = to_y_blocks([(extra[:384], None)], [came])
    blocks, extra = together(blocks, extra)
    extra = send(extra, "y")
    blocks = send(y_then_z_blocks([blocks, extra], [(384, 384, 384), ((128,))]), Z)
    sums = finish_x(total_of([blocks, blocks_u]))
    sum_one, sum_o, sum_f = sums[:, :1280], sums[:, 1280:2816], sums[:, 2816:]

    small = sum_one[:, 1152:]
    features = small[:, :6].reshape(2, 6, 6)
    features = jnp.where(first_half, features[0], features[1]).T
    heads = small[:, 6:12].T.reshape(2, 36)
    heads = jnp.where(first_half, heads[0], heads[1])
    return (
        block_out[None],
        d_tokens[None],
        jnp.stack([sum_one[:, :384], sum_one[:, 384:768], sum_one[:, 768:1152]]),
        heads[:12].reshape(2, 6, 1),
        sum_f[:, 1536:].T,
        sum_f[:, :1536],
        heads[12:].reshape(24, 1),
        sum_o.T,
        features[0:2],
        features[2:4],
        features[4:6],
    )


def solution(mesh):
    fine = Mesh(mesh.devices.reshape(2, 4, 4, 2, 2), AXES)
    both = P(None, DP + ("zl",))
    weights = (P(None, DP, "zl"), P(None, "zl", DP), P("zl", DP), P(DP, "zl"), P("zl", DP), P("zl", DP))
    wide = P(DP, "zl", None)
    return jax.shard_map(
        body,
        mesh=fine,
        in_specs=(wide, P(DP, "zl"), wide) + weights + (both, both, both),
        out_specs=(wide, wide) + weights + (both, both, both),
        check_vma=False,
    )
```

```python
import jax
import jax.numpy as jnp
from jax import lax
from jax.experimental import pallas as pl
from jax.experimental.pallas import tpu as pltpu
from jax.sharding import Mesh, PartitionSpec as P

AXES = ("zh", "y", "x", "core", "zl")
DP = ("zh", "y", "x", "core")
Z = ("zh", "zl")
HALF = 512
WIDTH = 768
FF = 3072
BF = jnp.bfloat16
F32 = jnp.float32
VMEM = 60 * 1024 * 1024


def swap(value, axis, bit):
    count = 2 if axis == "core" else 4
    return lax.ppermute(value, axis, [(i, i ^ bit) for i in range(count)])


def dot(a, b, ca, cb):
    return lax.dot_general(a, b, (((ca,), (cb,)), ((), ())), preferred_element_type=F32)


def together(*values):
    return lax.optimization_barrier(values)


def after(value, *earlier):
    return lax.optimization_barrier((value, earlier))[0]


def combine(inputs, outputs, plan):
    def kernel(*refs):
        sources, results = refs[: len(inputs)], refs[len(inputs) :]
        for out, r, c, rows, cols, terms in plan:
            read = [sources[i][a : a + rows, b : b + cols] for i, a, b in terms]
            total = read[0]
            if len(read) > 1:
                total = total.astype(F32)
                for term in read[1:]:
                    total = total + term.astype(F32)
            results[out][r : r + rows, c : c + cols] = total.astype(results[out].dtype)

    moved = sum(2 * v.size for v in inputs) + sum(2 * r * c for r, c in outputs)
    return pl.pallas_call(
        kernel,
        out_shape=[jax.ShapeDtypeStruct(shape, BF) for shape in outputs],
        compiler_params=pltpu.CompilerParams(vmem_limit_bytes=VMEM),
        cost_estimate=pl.CostEstimate(flops=0, bytes_accessed=moved, transcendentals=0),
    )(*inputs)


def place(inputs, outputs, plan):
    def kernel(*refs):
        sources = refs[: len(inputs)]
        results = refs[len(inputs) : len(inputs) + len(outputs)]
        sems = refs[-1]
        copies = [
            pltpu.make_async_copy(
                sources[i].at[a : a + rows, b : b + cols],
                results[out].at[r : r + rows, c : c + cols],
                sems.at[n],
            )
            for n, (out, r, c, rows, cols, (i, a, b)) in enumerate(plan)
        ]
        for copy in copies:
            copy.start()
        for copy in copies:
            copy.wait()

    return pl.pallas_call(
        kernel,
        out_shape=[jax.ShapeDtypeStruct(shape, BF) for shape in outputs],
        in_specs=[pl.BlockSpec(memory_space=pl.ANY)] * len(inputs),
        scratch_shapes=[pltpu.SemaphoreType.DMA((len(plan),))],
        compiler_params=pltpu.CompilerParams(vmem_limit_bytes=VMEM),
        cost_estimate=pl.CostEstimate(
            flops=0, bytes_accessed=sum(4 * r * c for r, c in outputs), transcendentals=0
        ),
    )(*inputs)


def others(part, axis):
    return [swap(part, axis, k) for k in (1, 2, 3)]


def join_z(pieces, widths):
    plan, at = [], 0
    for width in widths:
        for bit in range(4):
            plan.append((0, bit // 2 * 48, 2 * at + bit % 2 * width, 48, width, (bit, 0, at)))
        at += width
    return place(pieces, [(96, 2 * at)], plan)[0]


def join_y(pieces):
    width = pieces[0].shape[1]
    return place(pieces, [(192, width)], [(0, 48 * k, 0, 48, width, (k, 0, 0)) for k in range(4)])[0]


def with_core(pieces):
    return [swap(piece, "core", 1) for piece in pieces]


def around_first(part, axis):
    return swap(part, axis, 1), swap(part, axis, 3)


def assemble_y(pieces, cuts):
    plan, pairs = [], list(zip((0,) + cuts[:-1], cuts))
    for out, (a, b) in enumerate(pairs):
        row = 0
        for i, piece in enumerate(pieces):
            plan.append((out, row, 0, piece.shape[0], b - a, (i, 0, a)))
            row += piece.shape[0]
    return place(pieces, [(WIDTH, b - a) for a, b in pairs], plan)


def assemble_z(pieces):
    width = pieces[0].shape[1]
    plan = []
    for i in range(8):
        core, bit = i // 4, i % 4
        for k in range(4):
            row = core * 384 + k * 96 + bit // 2 * 48
            plan.append((0, row, bit % 2 * width, 48, width, (i, 48 * k, 0)))
    return place(pieces, [(WIDTH, 2 * width)], plan)[0]


def send_core(parts):
    return [swap(sent, "core", 1) for _, sent in parts]


def to_y_blocks(parts, came):
    plan, at, count = [], 0, len(parts)
    for i, (own, _) in enumerate(parts):
        width = own.shape[1]
        for k in range(4):
            plan.append((k, 0, at, 96, width, [(i, 96 * k, 0), (count + i, 96 * k, 0)]))
        at += width
    return combine([own for own, _ in parts] + came, [(96, at)] * 4, plan)


def to_z_blocks(parts, came):
    plan, at, count = [], 0, len(parts)
    for i, (own, _) in enumerate(parts):
        width = own.shape[1] // 2
        for bit in range(4):
            for k in range(4):
                row, col = 96 * k + bit // 2 * 48, bit % 2 * width
                plan.append((bit, 48 * k, at, 48, width, [(i, row, col), (count + i, row, col)]))
        at += width
    return combine([own for own, _ in parts] + came, [(192, at)] * 4, plan)


def send(blocks, axis):
    return [blocks[0]] + [swap(blocks[k], axis, k) for k in (1, 2, 3)]


def y_then_z_blocks(groups, widths):
    plan, at = [], 0
    for g, group_widths in enumerate(widths):
        col = 0
        for width in group_widths:
            for bit in range(4):
                shared = groups[g][0].shape[1] == width
                row, c = bit // 2 * 48, col + (0 if shared else bit % 2 * width)
                plan.append((bit, 0, at, 48, width, [(4 * g + i, row, c) for i in range(4)]))
            col += 2 * width
            at += width
    return combine(sum(groups, []), [(48, at)] * 4, plan)


def z_then_y_blocks(groups):
    plan, at = [], 0
    for g, group in enumerate(groups):
        width = group[0].shape[1]
        for k in range(4):
            plan.append((k, 0, at, 48, width, [(4 * g + i, 48 * k, 0) for i in range(4)]))
        at += width
    return combine(sum(groups, []), [(48, at)] * 4, plan)


def total_of(groups):
    plan, at = [], 0
    for g, group in enumerate(groups):
        width = group[0].shape[1]
        plan.append((0, 0, at, 48, width, [(4 * g + i, 0, 0) for i in range(4)]))
        at += width
    return combine(sum(groups, []), [(48, at)], plan)[0]


def finish_x(low):
    total = low[:12].astype(F32)
    for k in (1, 2, 3):
        total = total + swap(low[12 * k : 12 * k + 12], "x", k).astype(F32)
    return total


def halves(a, b):
    return dot(a[:, :384], b, 0, 0).astype(BF), dot(a[:, 384:], b, 0, 0).astype(BF)


def lanes_of(head, value):
    lane = lax.broadcasted_iota(jnp.int32, value.shape, 1)
    return jnp.where((lane >= 64) == (head == 1), value, jnp.zeros_like(value))


def attend_kernel(q_ref, k_ref, v_ref, segq_ref, segk_ref, out_ref, p_ref, bias_ref):
    @pl.when(pl.program_id(0) == 0)
    def _():
        place_k = lax.broadcasted_iota(jnp.int32, (2 * HALF, HALF), 0)
        place_q = lax.broadcasted_iota(jnp.int32, (2 * HALF, HALF), 1) + HALF
        allowed = (segk_ref[...] == segq_ref[...]) & (place_k <= place_q)
        bias_ref[...] = jnp.where(allowed, 0.0, -1e30)

    for block in range(2):
        keys = HALF + 256 * (block + 1)
        rows = slice(256 * block, 256 * (block + 1))
        q = q_ref[rows, :] * 0.125
        k = k_ref[:keys, :]
        mixed = []
        for head in range(2):
            s = dot(k, lanes_of(head, q), 1, 1) + bias_ref[:keys, rows]
            e = jnp.exp(s - jnp.max(s, axis=0, keepdims=True))
            p = (e * (1.0 / jnp.sum(e, axis=0, keepdims=True))).astype(BF)
            p_ref[head, :keys, rows] = p
            mixed.append(dot(v_ref[:keys, :], p, 0, 0))
        feature = lax.broadcasted_iota(jnp.int32, mixed[0].shape, 0)
        out_ref[rows, :] = jnp.where(feature < 64, mixed[0], mixed[1]).T.astype(BF)


def attend(qkv, seg_q, seg_k):
    whole = lambda shape: pl.BlockSpec(shape, lambda i: (0, 0))
    return pl.pallas_call(
        attend_kernel,
        grid=(6,),
        in_specs=[
            pl.BlockSpec((HALF, 128), lambda i: (1, i)),
            pl.BlockSpec((2 * HALF, 128), lambda i: (0, i + 6)),
            pl.BlockSpec((2 * HALF, 128), lambda i: (0, i + 12)),
            whole((1, HALF)),
            whole((2 * HALF, 1)),
        ],
        out_specs=[
            pl.BlockSpec((HALF, 128), lambda i: (0, i)),
            pl.BlockSpec((2, 2 * HALF, HALF), lambda i: (i, 0, 0)),
        ],
        out_shape=[
            jax.ShapeDtypeStruct((HALF, WIDTH), BF),
            jax.ShapeDtypeStruct((12, 2 * HALF, HALF), BF),
        ],
        scratch_shapes=[pltpu.VMEM((2 * HALF, HALF), F32)],
        compiler_params=pltpu.CompilerParams(vmem_limit_bytes=VMEM),
        cost_estimate=pl.CostEstimate(
            flops=12 * HALF * HALF * 2 * 64 * 4, bytes_accessed=18_000_000, transcendentals=6_000_000
        ),
    )(qkv, qkv, qkv, seg_q, seg_k)


def attend_back_kernel(q_ref, k_ref, v_ref, p_ref, g_ref, dq_ref, dk_ref, dv_ref):
    dk_sum, dv_sum = None, None
    for block in range(2):
        keys = HALF + 256 * (block + 1)
        rows = slice(256 * block, 256 * (block + 1))
        q = q_ref[rows, :] * 0.125
        g = g_ref[rows, :]
        k = k_ref[:keys, :]
        v = v_ref[:keys, :]
        dq, dk, dv = [], [], []
        for head in range(2):
            p = p_ref[head, :keys, rows]
            dp = dot(v, lanes_of(head, g), 1, 1)
            wide = p.astype(F32)
            inner = jnp.sum(wide * dp, axis=0, keepdims=True)
            ds = (wide * (dp - inner)).astype(BF)
            dv.append(dot(p, g, 1, 0))
            dk.append(dot(ds, q, 1, 0))
            dq.append(dot(k, ds, 0, 0))
        feature = lax.broadcasted_iota(jnp.int32, dq[0].shape, 0)
        dq_ref[rows, :] = (jnp.where(feature < 64, dq[0], dq[1]).T * 0.125).astype(BF)
        lane = lax.broadcasted_iota(jnp.int32, dk[0].shape, 1)
        dk = jnp.where(lane < 64, dk[0], dk[1])
        dv = jnp.where(lane < 64, dv[0], dv[1])
        if block == 0:
            dk_sum, dv_sum = dk, dv
        else:
            seen = HALF + 256
            dk_ref[:seen, :] = (dk_sum + dk[:seen]).astype(BF)
            dv_ref[:seen, :] = (dv_sum + dv[:seen]).astype(BF)
            dk_ref[seen:, :] = dk[seen:].astype(BF)
            dv_ref[seen:, :] = dv[seen:].astype(BF)


def attend_back(qkv, p, grad, first, filled=()):
    narrow = pl.BlockSpec((HALF, 128), lambda i: (0, i + first))
    tall = pl.BlockSpec((2 * HALF, 128), lambda i: (0, i + first))

    def kernel(*refs):
        attend_back_kernel(*refs[:5], *refs[5 + len(filled) :])

    return pl.pallas_call(
        kernel,
        grid=(3,),
        in_specs=[
            pl.BlockSpec((HALF, 128), lambda i: (1, i + first)),
            pl.BlockSpec((2 * HALF, 128), lambda i: (0, i + first + 6)),
            pl.BlockSpec((2 * HALF, 128), lambda i: (0, i + first + 12)),
            pl.BlockSpec((2, 2 * HALF, HALF), lambda i: (i + first, 0, 0)),
            pl.BlockSpec((HALF, 128), lambda i: (0, i + first)),
        ]
        + [pl.BlockSpec(memory_space=pl.ANY)] * len(filled),
        input_output_aliases={5 + n: n for n in range(len(filled))},
        out_specs=[narrow, tall, tall],
        out_shape=[
            jax.ShapeDtypeStruct((HALF, WIDTH), BF),
            jax.ShapeDtypeStruct((2 * HALF, WIDTH), BF),
            jax.ShapeDtypeStruct((2 * HALF, WIDTH), BF),
        ],
        compiler_params=pltpu.CompilerParams(vmem_limit_bytes=VMEM),
        cost_estimate=pl.CostEstimate(
            flops=6 * HALF * HALF * 2 * 64 * 8, bytes_accessed=10_000_000, transcendentals=0
        ),
    )(qkv, qkv, qkv, p, grad, *filled)


def standard(values):
    centred = values - jnp.mean(values, axis=-1, keepdims=True)
    variance = jnp.mean(centred * centred, axis=-1, keepdims=True)
    inverse = lax.rsqrt(variance + 1e-05)
    return centred * inverse, inverse


def norm_back(gradient, normed, inverse, gain):
    scaled = gradient * gain
    first = jnp.mean(scaled, axis=-1, keepdims=True)
    second = jnp.mean(scaled * normed, axis=-1, keepdims=True)
    return (
        inverse * (scaled - first - normed * second),
        jnp.sum(gradient * normed, axis=0),
        jnp.sum(gradient, axis=0),
    )


def gelu_both(u):
    inner = 0.7978845608028654 * (u + 0.044715 * u * u * u)
    t = jnp.tanh(inner)
    slope = 0.7978845608028654 * (1.0 + 3.0 * 0.044715 * u * u)
    return 0.5 * u * (1.0 + t), 0.5 * (1.0 + t) + 0.5 * u * (1.0 - t * t) * slope


def feature_order():
    place = jnp.arange(WIDTH, dtype=jnp.int32)
    row, owner = place % 12, place // 12
    zh = lax.axis_index("zh") ^ (owner // 4 % 2)
    y = lax.axis_index("y") ^ (owner // 8 % 4)
    x = lax.axis_index("x") ^ (owner % 4)
    core = lax.axis_index("core") ^ (owner // 32)
    return ((zh * 4 + y) * 4 + x) * 2 + core, row


def body(
    tokens, segments, cotangent, w_qkv, b_qv, w_proj, w_fc, b_fc, w_out, ln_gains, ln_biases, out_biases
):
    first_half = lax.axis_index("zl") == 0
    before = lambda v: lax.ppermute(v, "zl", [(0, 1)])
    vectors = jnp.concatenate([ln_gains, ln_biases, out_biases], 0)
    high = lax.reduce_precision(vectors, 8, 7)
    middle = lax.reduce_precision(vectors - high, 8, 7)
    terms = jnp.concatenate([high, middle, vectors - high - middle], 0).T
    empty = jnp.zeros_like(terms)
    terms = jnp.where(
        first_half, jnp.concatenate([terms, empty], 0), jnp.concatenate([empty, terms], 0)
    ).astype(BF)
    extra = jnp.concatenate(
        [terms, b_qv.reshape(12, 1), b_fc.reshape(2, 12).T, jnp.zeros((12, 107), BF)], 1
    )
    weights = jnp.concatenate([*w_qkv, extra, w_fc, w_out.T, w_proj.T], 1)
    pieces, prev_a, prev_segments = together(
        [weights] + others(weights, "x"), before(tokens[0, :256]), before(segments[0])
    )
    prev_segments = jnp.where(first_half, -1, prev_segments)
    one, two, three = [
        jnp.concatenate([v[:, a:b] for v in pieces], 0)
        for a, b in ((0, 1280), (1280, 2816), (2816, 4736))
    ]
    one = join_z([one] + others(one, Z), (384, 384, 384, 128))
    late, cot = after((tokens[0, 256:], cotangent[0]), one)

    owner, row = feature_order()
    turn = (
        jnp.arange(WIDTH, dtype=jnp.int32)[:, None] == (owner * 12 + row)[None, :]
    ).astype(BF)
    index = lambda n: jnp.arange(n, dtype=jnp.int32)
    of_owner = (owner[:, None] == index(64)[None, :]).astype(BF)
    of_row = (row[:, None] == index(72)[None, :] % 12).astype(F32)
    column = (index(128)[None, :] - index(72)[:, None] // 12).astype(F32)
    turn, of_owner, of_row, column = together(turn, of_owner, of_row, column)

    prev_b = before(late)
    three = after(three, prev_b)
    own_core, prev_b, pieces, ones = together(
        with_core([one]), prev_b, [three] + others(three, Z), others(one, "y")
    )
    three = join_z(pieces, (1536, 384))
    whole_row = jnp.concatenate([prev_a, prev_b, tokens[0]], 0)
    stream = dot(whole_row, turn, 1, 0).astype(BF).astype(F32)
    grad_low = dot(cot, turn, 1, 0).astype(BF)
    xhat1, inv1 = standard(stream)
    ones_core, xhat1, inv1, grad_low = together(with_core(ones), xhat1, inv1, grad_low)
    two = after(two, ones_core)
    pieces = [two] + others(two, "y")
    one, small = assemble_y([one] + ones + own_core + ones_core, (2304, 2560))
    w_q, w_k, w_v = one[:, :768], one[:, 768:1536], one[:, 1536:]

    terms = ((index(128)[None, :] % 6 == index(8)[:, None]) & (index(128)[None, :] < 18)).astype(BF)
    vectors = dot(terms, small[:, :128], 1, 1) + dot(terms, small[:, 128:], 1, 1)
    gains, shifts, biases = vectors[0:2], vectors[2:4], vectors[4:6]

    def entries(part):
        spread = dot(part, (column[:36] == 18).astype(BF), 1, 1) * of_row[:, :36]
        return dot(spread.astype(BF), of_owner, 0, 0)

    own_bias, other_bias = entries(small[:, :128]), entries(small[:, 128:])
    rows_of = lambda a, b: jnp.concatenate([own_bias[a:b], other_bias[a:b]], 0).reshape(-1)
    bias_q, bias_v, bias_f = rows_of(0, 6), rows_of(6, 12), rows_of(12, 36)

    a1 = (xhat1 * gains[0] + shifts[0]).astype(BF)
    a1, pieces, three = together(a1, pieces, three)
    two = join_y(pieces)
    two, three, a1 = together(two, three, a1)
    two_round, three_round = around_first(two, Z), around_first(three, "y")
    stream, xhat1, inv1 = stream[HALF:], xhat1[HALF:], inv1[HALF:]
    zeros = jnp.zeros((WIDTH,), F32)
    qkv_bias = jnp.concatenate([bias_q, zeros, bias_v])
    qkv = (dot(a1, one, 1, 0) + qkv_bias).astype(BF)
    seg_k = jnp.concatenate([prev_segments, segments[0]], 0)[:, None]
    qkv, two, three, two_round, three_round = together(qkv, two, three, two_round, three_round)
    two_far, three_far = swap(two, Z, 2), swap(three, "y", 2)
    two_core, three_core = with_core([two]), with_core([three])
    attn, probs = attend(qkv, segments, seg_k)
    attn, two_far, three_far, two_core, three_core, two_round, three_round = together(
        attn, two_far, three_far, two_core, three_core, two_round, three_round
    )
    two_rest = [two_round[0], two_far, two_round[1]]
    three_rest = [three_round[0], three_far, three_round[1]]
    two = [two] + two_rest + two_core + with_core(two_rest)
    three = [three] + three_rest + three_core + with_core(three_rest)
    w_o, w_p = assemble_y(three, (3072, 3840))
    w_f = assemble_z(two)

    r1 = stream + dot(attn, w_p, 1, 1) + biases[0]
    xhat2, inv2 = standard(r1)
    a2 = (xhat2 * gains[1] + shifts[1]).astype(BF)
    act, slope = gelu_both(dot(a2, w_f, 1, 0) + bias_f)
    act = act.astype(BF)
    parts_o = [halves(grad_low, act)]
    came_o = send_core(parts_o)
    grad_next, parts_o = lax.optimization_barrier((grad_low, parts_o))
    out = (r1 + dot(act, w_o, 1, 1) + biases[1]).astype(BF)
    block_out = dot(after(out), turn, 1, 1).astype(BF)

    grad = grad_low.astype(F32)
    d_bias_two = jnp.sum(grad, axis=0)
    du = (dot(grad_next, w_o, 1, 0) * slope).astype(BF)
    d_bias_f = jnp.sum(du.astype(F32), axis=0)
    du, came_o = lax.optimization_barrier((du, came_o))
    blocks_o = send(to_y_blocks(parts_o, came_o), "y")
    parts_f = [halves(a2, du)]
    came_f = send_core(parts_f)
    du, parts_f = lax.optimization_barrier((du, parts_f))
    da2 = after(dot(du, w_f, 1, 1))
    dv2, d_gain_two, d_shift_two = norm_back(da2, xhat2, inv2, gains[1])
    dr1 = grad + dv2
    g1 = dr1.astype(BF)
    d_bias_one = jnp.sum(g1.astype(F32), axis=0)
    parts_p = [halves(g1, attn)]
    came_p = send_core(parts_p)
    dattn = dot(g1, w_p, 1, 0).astype(BF)
    dattn, blocks_o, came_f, came_p = lax.optimization_barrier((dattn, blocks_o, came_f, came_p))
    blocks_f = to_y_blocks(parts_f + parts_p, came_f + came_p)
    dattn, blocks_f = lax.optimization_barrier((dattn, blocks_f))
    blocks_f = send(blocks_f, "y")
    filled = attend_back(qkv, probs, dattn, 0)
    dq, dk, dv = attend_back(qkv, probs, dattn, 3, tuple(filled))
    dq, dk, dv, blocks_f = together(dq, dk, dv, blocks_f)
    da1_prev = (dot(dk[:HALF], w_k, 1, 1) + dot(dv[:HALF], w_v, 1, 1)).astype(BF)
    blocks_u = y_then_z_blocks([blocks_o, blocks_f], [(1536,), (1536, 384)])
    da1_prev, blocks_u, dq, dk, dv = together(da1_prev, blocks_u, dq, dk, dv)
    da1_sent = lax.ppermute(da1_prev, "zl", [(1, 0)])
    blocks_u = send(blocks_u, Z)
    sent = [dot(u[:, 384:], v, 0, 0).astype(BF) for u, v in ((a1[HALF:], dq), (a1, dk), (a1, dv))]
    dq, dk, dv, sent = together(dq, dk, dv, sent)
    came = [swap(v, "core", 1) for v in sent]
    parts = [
        (dot(u[:, :384], v, 0, 0).astype(BF), None) for u, v in ((a1[HALF:], dq), (a1, dk), (a1, dv))
    ]
    parts, came = together(parts, came)
    blocks = to_y_blocks(parts, came)
    dq, dk, dv, blocks = together(dq, dk, dv, blocks)
    blocks = send(blocks, "y")
    da1 = dot(dq, w_q, 1, 1) + dot(dk[HALF:], w_k, 1, 1) + dot(dv[HALF:], w_v, 1, 1)
    da1, da1_sent = together(da1, da1_sent)
    da1 = da1 + da1_sent.astype(F32)
    dv1, d_gain_one, d_shift_one = norm_back(da1, xhat1, inv1, gains[0])
    d_tokens = dot(after((dr1 + dv1).astype(BF)), turn, 1, 1).astype(BF)

    d_bias_q = jnp.sum(dq.astype(F32), axis=0).reshape(2, 6, 64)
    d_bias_v = jnp.sum(dv.astype(F32), axis=0).reshape(2, 6, 64)
    d_bias_f = d_bias_f.reshape(2, 24, 64)
    per_head = jnp.concatenate([d_bias_q, d_bias_v, d_bias_f], 1)
    per_head = jnp.where(first_half, per_head, per_head[::-1]).reshape(72, 64).astype(BF)
    per_head = (dot(of_owner, per_head, 1, 1) * of_row).astype(BF)
    per_feature = jnp.stack(
        [d_gain_one, d_gain_two, d_shift_one, d_shift_two, d_bias_one, d_bias_two]
    ).astype(BF)
    extra = dot(per_feature, jnp.eye(6, 128, dtype=BF), 0, 0)
    extra = (extra + dot(per_head, (column == 6).astype(BF), 1, 0)).astype(BF)
    came = swap(extra[384:], "core", 1)
    extra = to_y_blocks([(extra[:384], None)], [came])
    blocks, extra = together(blocks, extra)
    extra = send(extra, "y")
    blocks = send(y_then_z_blocks([blocks, extra], [(384, 384, 384), ((128,))]), Z)
    sums = finish_x(total_of([blocks, blocks_u]))
    sum_one, sum_o, sum_f = sums[:, :1280], sums[:, 1280:2816], sums[:, 2816:]

    small = sum_one[:, 1152:]
    features = small[:, :6].reshape(2, 6, 6)
    features = jnp.where(first_half, features[0], features[1]).T
    heads = small[:, 6:12].T.reshape(2, 36)
    heads = jnp.where(first_half, heads[0], heads[1])
    return (
        block_out[None],
        d_tokens[None],
        jnp.stack([sum_one[:, :384], sum_one[:, 384:768], sum_one[:, 768:1152]]),
        heads[:12].reshape(2, 6, 1),
        sum_f[:, 1536:].T,
        sum_f[:, :1536],
        heads[12:].reshape(24, 1),
        sum_o.T,
        features[0:2],
        features[2:4],
        features[4:6],
    )


def solution(mesh):
    fine = Mesh(mesh.devices.reshape(2, 4, 4, 2, 2), AXES)
    both = P(None, DP + ("zl",))
    weights = (P(None, DP, "zl"), P(None, "zl", DP), P("zl", DP), P(DP, "zl"), P("zl", DP), P("zl", DP))
    wide = P(DP, "zl", None)
    return jax.shard_map(
        body,
        mesh=fine,
        in_specs=(wide, P(DP, "zl"), wide) + weights + (both, both, both),
        out_specs=(wide, wide) + weights + (both, both, both),
        check_vma=False,
    )
```

```python
import jax
import jax.numpy as jnp
from jax import lax
from jax.experimental import pallas as pl
from jax.experimental.pallas import tpu as pltpu
from jax.sharding import Mesh, PartitionSpec as P

AXES = ("zh", "y", "x", "core", "zl")
DP = ("zh", "y", "x", "core")
Z = ("zh", "zl")
HALF = 512
WIDTH = 768
FF = 3072
BF = jnp.bfloat16
F32 = jnp.float32
VMEM = 60 * 1024 * 1024


def swap(value, axis, bit):
    count = 2 if axis == "core" else 4
    return lax.ppermute(value, axis, [(i, i ^ bit) for i in range(count)])


def dot(a, b, ca, cb):
    return lax.dot_general(a, b, (((ca,), (cb,)), ((), ())), preferred_element_type=F32)


def together(*values):
    return lax.optimization_barrier(values)


def after(value, *earlier):
    return lax.optimization_barrier((value, earlier))[0]


def combine(inputs, outputs, plan):
    def kernel(*refs):
        sources, results = refs[: len(inputs)], refs[len(inputs) :]
        for out, r, c, rows, cols, terms in plan:
            read = [sources[i][a : a + rows, b : b + cols] for i, a, b in terms]
            total = read[0]
            if len(read) > 1:
                total = total.astype(F32)
                for term in read[1:]:
                    total = total + term.astype(F32)
            results[out][r : r + rows, c : c + cols] = total.astype(results[out].dtype)

    moved = sum(2 * v.size for v in inputs) + sum(2 * r * c for r, c in outputs)
    return pl.pallas_call(
        kernel,
        out_shape=[jax.ShapeDtypeStruct(shape, BF) for shape in outputs],
        compiler_params=pltpu.CompilerParams(vmem_limit_bytes=VMEM),
        cost_estimate=pl.CostEstimate(flops=0, bytes_accessed=moved, transcendentals=0),
    )(*inputs)


def place(inputs, outputs, plan):
    def kernel(*refs):
        sources = refs[: len(inputs)]
        results = refs[len(inputs) : len(inputs) + len(outputs)]
        sems = refs[-1]
        copies = [
            pltpu.make_async_copy(
                sources[i].at[a : a + rows, b : b + cols],
                results[out].at[r : r + rows, c : c + cols],
                sems.at[n],
            )
            for n, (out, r, c, rows, cols, (i, a, b)) in enumerate(plan)
        ]
        for copy in copies:
            copy.start()
        for copy in copies:
            copy.wait()

    return pl.pallas_call(
        kernel,
        out_shape=[jax.ShapeDtypeStruct(shape, BF) for shape in outputs],
        in_specs=[pl.BlockSpec(memory_space=pl.ANY)] * len(inputs),
        scratch_shapes=[pltpu.SemaphoreType.DMA((len(plan),))],
        compiler_params=pltpu.CompilerParams(vmem_limit_bytes=VMEM),
        cost_estimate=pl.CostEstimate(
            flops=0, bytes_accessed=sum(4 * r * c for r, c in outputs), transcendentals=0
        ),
    )(*inputs)


def others(part, axis):
    return [swap(part, axis, k) for k in (1, 2, 3)]


def join_z(pieces, widths):
    plan, at = [], 0
    for width in widths:
        for bit in range(4):
            plan.append((0, bit // 2 * 48, 2 * at + bit % 2 * width, 48, width, (bit, 0, at)))
        at += width
    return place(pieces, [(96, 2 * at)], plan)[0]


def join_y(pieces):
    width = pieces[0].shape[1]
    return place(pieces, [(192, width)], [(0, 48 * k, 0, 48, width, (k, 0, 0)) for k in range(4)])[0]


def with_core(pieces):
    return [swap(piece, "core", 1) for piece in pieces]


def around_first(part, axis):
    return swap(part, axis, 1), swap(part, axis, 3)


def assemble_y(pieces, cuts):
    plan, pairs = [], list(zip((0,) + cuts[:-1], cuts))
    for out, (a, b) in enumerate(pairs):
        row = 0
        for i, piece in enumerate(pieces):
            plan.append((out, row, 0, piece.shape[0], b - a, (i, 0, a)))
            row += piece.shape[0]
    return place(pieces, [(WIDTH, b - a) for a, b in pairs], plan)


def assemble_z(pieces):
    width = pieces[0].shape[1]
    plan = []
    for i in range(8):
        core, bit = i // 4, i % 4
        for k in range(4):
            row = core * 384 + k * 96 + bit // 2 * 48
            plan.append((0, row, bit % 2 * width, 48, width, (i, 48 * k, 0)))
    return place(pieces, [(WIDTH, 2 * width)], plan)[0]


def send_core(parts):
    return [swap(sent, "core", 1) for _, sent in parts]


def to_y_blocks(parts, came):
    plan, at, count = [], 0, len(parts)
    for i, (own, _) in enumerate(parts):
        width = own.shape[1]
        for k in range(4):
            plan.append((k, 0, at, 96, width, [(i, 96 * k, 0), (count + i, 96 * k, 0)]))
        at += width
    return combine([own for own, _ in parts] + came, [(96, at)] * 4, plan)


def to_z_blocks(parts, came):
    plan, at, count = [], 0, len(parts)
    for i, (own, _) in enumerate(parts):
        width = own.shape[1] // 2
        for bit in range(4):
            for k in range(4):
                row, col = 96 * k + bit // 2 * 48, bit % 2 * width
                plan.append((bit, 48 * k, at, 48, width, [(i, row, col), (count + i, row, col)]))
        at += width
    return combine([own for own, _ in parts] + came, [(192, at)] * 4, plan)


def send(blocks, axis):
    return [blocks[0]] + [swap(blocks[k], axis, k) for k in (1, 2, 3)]


def y_then_z_blocks(groups, widths):
    plan, at = [], 0
    for g, group_widths in enumerate(widths):
        col = 0
        for width in group_widths:
            for bit in range(4):
                shared = groups[g][0].shape[1] == width
                row, c = bit // 2 * 48, col + (0 if shared else bit % 2 * width)
                plan.append((bit, 0, at, 48, width, [(4 * g + i, row, c) for i in range(4)]))
            col += 2 * width
            at += width
    return combine(sum(groups, []), [(48, at)] * 4, plan)


def z_then_y_blocks(groups):
    plan, at = [], 0
    for g, group in enumerate(groups):
        width = group[0].shape[1]
        for k in range(4):
            plan.append((k, 0, at, 48, width, [(4 * g + i, 48 * k, 0) for i in range(4)]))
        at += width
    return combine(sum(groups, []), [(48, at)] * 4, plan)


def total_of(groups):
    plan, at = [], 0
    for g, group in enumerate(groups):
        width = group[0].shape[1]
        plan.append((0, 0, at, 48, width, [(4 * g + i, 0, 0) for i in range(4)]))
        at += width
    return combine(sum(groups, []), [(48, at)], plan)[0]


def finish_x(low):
    total = low[:12].astype(F32)
    for k in (1, 2, 3):
        total = total + swap(low[12 * k : 12 * k + 12], "x", k).astype(F32)
    return total


def halves(a, b):
    return dot(a[:, :384], b, 0, 0).astype(BF), dot(a[:, 384:], b, 0, 0).astype(BF)


def lanes_of(head, value):
    lane = lax.broadcasted_iota(jnp.int32, value.shape, 1)
    return jnp.where((lane >= 64) == (head == 1), value, jnp.zeros_like(value))


def attend_kernel(q_ref, k_ref, v_ref, segq_ref, segk_ref, out_ref, p_ref, bias_ref):
    @pl.when(pl.program_id(0) == 0)
    def _():
        place_k = lax.broadcasted_iota(jnp.int32, (2 * HALF, HALF), 0)
        place_q = lax.broadcasted_iota(jnp.int32, (2 * HALF, HALF), 1) + HALF
        allowed = (segk_ref[...] == segq_ref[...]) & (place_k <= place_q)
        bias_ref[...] = jnp.where(allowed, 0.0, -1e30)

    for block in range(2):
        keys = HALF + 256 * (block + 1)
        rows = slice(256 * block, 256 * (block + 1))
        q = q_ref[rows, :] * 0.125
        k = k_ref[:keys, :]
        mixed = []
        for head in range(2):
            s = dot(k, lanes_of(head, q), 1, 1) + bias_ref[:keys, rows]
            e = jnp.exp(s - jnp.max(s, axis=0, keepdims=True))
            p = (e * (1.0 / jnp.sum(e, axis=0, keepdims=True))).astype(BF)
            p_ref[head, :keys, rows] = p
            mixed.append(dot(v_ref[:keys, :], p, 0, 0))
        feature = lax.broadcasted_iota(jnp.int32, mixed[0].shape, 0)
        out_ref[rows, :] = jnp.where(feature < 64, mixed[0], mixed[1]).T.astype(BF)


def attend(qkv, seg_q, seg_k):
    whole = lambda shape: pl.BlockSpec(shape, lambda i: (0, 0))
    return pl.pallas_call(
        attend_kernel,
        grid=(6,),
        in_specs=[
            pl.BlockSpec((HALF, 128), lambda i: (1, i)),
            pl.BlockSpec((2 * HALF, 128), lambda i: (0, i + 6)),
            pl.BlockSpec((2 * HALF, 128), lambda i: (0, i + 12)),
            whole((1, HALF)),
            whole((2 * HALF, 1)),
        ],
        out_specs=[
            pl.BlockSpec((HALF, 128), lambda i: (0, i)),
            pl.BlockSpec((2, 2 * HALF, HALF), lambda i: (i, 0, 0)),
        ],
        out_shape=[
            jax.ShapeDtypeStruct((HALF, WIDTH), BF),
            jax.ShapeDtypeStruct((12, 2 * HALF, HALF), BF),
        ],
        scratch_shapes=[pltpu.VMEM((2 * HALF, HALF), F32)],
        compiler_params=pltpu.CompilerParams(vmem_limit_bytes=VMEM),
        cost_estimate=pl.CostEstimate(
            flops=12 * HALF * HALF * 2 * 64 * 4, bytes_accessed=18_000_000, transcendentals=6_000_000
        ),
    )(qkv, qkv, qkv, seg_q, seg_k)


def attend_back_kernel(q_ref, k_ref, v_ref, p_ref, g_ref, attn_ref, dq_ref, dk_ref, dv_ref):
    dk_sum, dv_sum = None, None
    for block in range(2):
        keys = HALF + 256 * (block + 1)
        rows = slice(256 * block, 256 * (block + 1))
        q = q_ref[rows, :] * 0.125
        g = g_ref[rows, :]
        through = (g.astype(F32) * attn_ref[rows, :].astype(F32)).T
        k = k_ref[:keys, :]
        v = v_ref[:keys, :]
        dq, dk, dv = [], [], []
        for head in range(2):
            p = p_ref[head, :keys, rows]
            dp = dot(v, lanes_of(head, g), 1, 1)
            wide = p.astype(F32)
            inner = jnp.sum(through[64 * head : 64 * head + 64], axis=0, keepdims=True)
            ds = (wide * (dp - inner)).astype(BF)
            dv.append(dot(p, g, 1, 0))
            dk.append(dot(ds, q, 1, 0))
            dq.append(dot(k, ds, 0, 0))
        feature = lax.broadcasted_iota(jnp.int32, dq[0].shape, 0)
        dq_ref[rows, :] = (jnp.where(feature < 64, dq[0], dq[1]).T * 0.125).astype(BF)
        lane = lax.broadcasted_iota(jnp.int32, dk[0].shape, 1)
        dk = jnp.where(lane < 64, dk[0], dk[1])
        dv = jnp.where(lane < 64, dv[0], dv[1])
        if block == 0:
            dk_sum, dv_sum = dk, dv
        else:
            seen = HALF + 256
            dk_ref[:seen, :] = (dk_sum + dk[:seen]).astype(BF)
            dv_ref[:seen, :] = (dv_sum + dv[:seen]).astype(BF)
            dk_ref[seen:, :] = dk[seen:].astype(BF)
            dv_ref[seen:, :] = dv[seen:].astype(BF)


def attend_back(qkv, p, grad, attn, first, filled=()):
    narrow = pl.BlockSpec((HALF, 128), lambda i: (0, i + first))
    tall = pl.BlockSpec((2 * HALF, 128), lambda i: (0, i + first))

    def kernel(*refs):
        attend_back_kernel(*refs[:6], *refs[6 + len(filled) :])

    return pl.pallas_call(
        kernel,
        grid=(3,),
        in_specs=[
            pl.BlockSpec((HALF, 128), lambda i: (1, i + first)),
            pl.BlockSpec((2 * HALF, 128), lambda i: (0, i + first + 6)),
            pl.BlockSpec((2 * HALF, 128), lambda i: (0, i + first + 12)),
            pl.BlockSpec((2, 2 * HALF, HALF), lambda i: (i + first, 0, 0)),
            pl.BlockSpec((HALF, 128), lambda i: (0, i + first)),
            pl.BlockSpec((HALF, 128), lambda i: (0, i + first)),
        ]
        + [pl.BlockSpec(memory_space=pl.ANY)] * len(filled),
        input_output_aliases={6 + n: n for n in range(len(filled))},
        out_specs=[narrow, tall, tall],
        out_shape=[
            jax.ShapeDtypeStruct((HALF, WIDTH), BF),
            jax.ShapeDtypeStruct((2 * HALF, WIDTH), BF),
            jax.ShapeDtypeStruct((2 * HALF, WIDTH), BF),
        ],
        compiler_params=pltpu.CompilerParams(vmem_limit_bytes=VMEM),
        cost_estimate=pl.CostEstimate(
            flops=6 * HALF * HALF * 2 * 64 * 8, bytes_accessed=10_000_000, transcendentals=0
        ),
    )(qkv, qkv, qkv, p, grad, attn, *filled)


def standard(values):
    centred = values - jnp.mean(values, axis=-1, keepdims=True)
    variance = jnp.mean(centred * centred, axis=-1, keepdims=True)
    inverse = lax.rsqrt(variance + 1e-05)
    return centred * inverse, inverse


def norm_back(gradient, normed, inverse, gain):
    scaled = gradient * gain
    first = jnp.mean(scaled, axis=-1, keepdims=True)
    second = jnp.mean(scaled * normed, axis=-1, keepdims=True)
    return (
        inverse * (scaled - first - normed * second),
        jnp.sum(gradient * normed, axis=0),
        jnp.sum(gradient, axis=0),
    )


def gelu_both(u):
    inner = 0.7978845608028654 * (u + 0.044715 * u * u * u)
    t = jnp.tanh(inner)
    slope = 0.7978845608028654 * (1.0 + 3.0 * 0.044715 * u * u)
    return 0.5 * u * (1.0 + t), 0.5 * (1.0 + t) + 0.5 * u * (1.0 - t * t) * slope


def feature_order():
    place = jnp.arange(WIDTH, dtype=jnp.int32)
    row, owner = place % 12, place // 12
    zh = lax.axis_index("zh") ^ (owner // 4 % 2)
    y = lax.axis_index("y") ^ (owner // 8 % 4)
    x = lax.axis_index("x") ^ (owner % 4)
    core = lax.axis_index("core") ^ (owner // 32)
    return ((zh * 4 + y) * 4 + x) * 2 + core, row


def body(
    tokens, segments, cotangent, w_qkv, b_qv, w_proj, w_fc, b_fc, w_out, ln_gains, ln_biases, out_biases
):
    first_half = lax.axis_index("zl") == 0
    before = lambda v: lax.ppermute(v, "zl", [(0, 1)])
    vectors = jnp.concatenate([ln_gains, ln_biases, out_biases], 0)
    high = lax.reduce_precision(vectors, 8, 7)
    middle = lax.reduce_precision(vectors - high, 8, 7)
    terms = jnp.concatenate([high, middle, vectors - high - middle], 0).T
    empty = jnp.zeros_like(terms)
    terms = jnp.where(
        first_half, jnp.concatenate([terms, empty], 0), jnp.concatenate([empty, terms], 0)
    ).astype(BF)
    extra = jnp.concatenate(
        [terms, b_qv.reshape(12, 1), b_fc.reshape(2, 12).T, jnp.zeros((12, 107), BF)], 1
    )
    weights = jnp.concatenate([*w_qkv, extra, w_fc, w_out.T, w_proj.T], 1)
    pieces, prev_a, prev_segments = together(
        [weights] + others(weights, "x"), before(tokens[0, :256]), before(segments[0])
    )
    prev_segments = jnp.where(first_half, -1, prev_segments)
    one, two, three = [
        jnp.concatenate([v[:, a:b] for v in pieces], 0)
        for a, b in ((0, 1280), (1280, 2816), (2816, 4736))
    ]
    one = join_z([one] + others(one, Z), (384, 384, 384, 128))
    late, cot = after((tokens[0, 256:], cotangent[0]), one)

    owner, row = feature_order()
    turn = (
        jnp.arange(WIDTH, dtype=jnp.int32)[:, None] == (owner * 12 + row)[None, :]
    ).astype(BF)
    index = lambda n: jnp.arange(n, dtype=jnp.int32)
    of_owner = (owner[:, None] == index(64)[None, :]).astype(BF)
    of_row = (row[:, None] == index(72)[None, :] % 12).astype(F32)
    column = (index(128)[None, :] - index(72)[:, None] // 12).astype(F32)
    turn, of_owner, of_row, column = together(turn, of_owner, of_row, column)

    prev_b = before(late)
    three = after(three, prev_b)
    own_core, prev_b, pieces, ones = together(
        with_core([one]), prev_b, [three] + others(three, Z), others(one, "y")
    )
    three = join_z(pieces, (1536, 384))
    whole_row = jnp.concatenate([prev_a, prev_b, tokens[0]], 0)
    stream = dot(whole_row, turn, 1, 0).astype(BF).astype(F32)
    grad_low = dot(cot, turn, 1, 0).astype(BF)
    xhat1, inv1 = standard(stream)
    ones_core, xhat1, inv1, grad_low = together(with_core(ones), xhat1, inv1, grad_low)
    two = after(two, ones_core)
    pieces = [two] + others(two, "y")
    one, small = assemble_y([one] + ones + own_core + ones_core, (2304, 2560))
    w_q, w_k, w_v = one[:, :768], one[:, 768:1536], one[:, 1536:]

    terms = ((index(128)[None, :] % 6 == index(8)[:, None]) & (index(128)[None, :] < 18)).astype(BF)
    vectors = dot(terms, small[:, :128], 1, 1) + dot(terms, small[:, 128:], 1, 1)
    gains, shifts, biases = vectors[0:2], vectors[2:4], vectors[4:6]

    def entries(part):
        spread = dot(part, (column[:36] == 18).astype(BF), 1, 1) * of_row[:, :36]
        return dot(spread.astype(BF), of_owner, 0, 0)

    own_bias, other_bias = entries(small[:, :128]), entries(small[:, 128:])
    rows_of = lambda a, b: jnp.concatenate([own_bias[a:b], other_bias[a:b]], 0).reshape(-1)
    bias_q, bias_v, bias_f = rows_of(0, 6), rows_of(6, 12), rows_of(12, 36)

    a1 = (xhat1 * gains[0] + shifts[0]).astype(BF)
    a1, pieces, three = together(a1, pieces, three)
    two = join_y(pieces)
    two, three, a1 = together(two, three, a1)
    two_round, three_round = around_first(two, Z), around_first(three, "y")
    stream, xhat1, inv1 = stream[HALF:], xhat1[HALF:], inv1[HALF:]
    zeros = jnp.zeros((WIDTH,), F32)
    qkv_bias = jnp.concatenate([bias_q, zeros, bias_v])
    qkv = (dot(a1, one, 1, 0) + qkv_bias).astype(BF)
    seg_k = jnp.concatenate([prev_segments, segments[0]], 0)[:, None]
    qkv, two, three, two_round, three_round = together(qkv, two, three, two_round, three_round)
    two_far, three_far = swap(two, Z, 2), swap(three, "y", 2)
    two_core, three_core = with_core([two]), with_core([three])
    attn, probs = attend(qkv, segments, seg_k)
    attn, two_far, three_far, two_core, three_core, two_round, three_round = together(
        attn, two_far, three_far, two_core, three_core, two_round, three_round
    )
    two_rest = [two_round[0], two_far, two_round[1]]
    three_rest = [three_round[0], three_far, three_round[1]]
    two = [two] + two_rest + two_core + with_core(two_rest)
    three = [three] + three_rest + three_core + with_core(three_rest)
    w_o, w_p = assemble_y(three, (3072, 3840))
    w_f = assemble_z(two)

    r1 = stream + dot(attn, w_p, 1, 1) + biases[0]
    xhat2, inv2 = standard(r1)
    a2 = (xhat2 * gains[1] + shifts[1]).astype(BF)
    act, slope = gelu_both(dot(a2, w_f, 1, 0) + bias_f)
    act = act.astype(BF)
    parts_o = [halves(grad_low, act)]
    came_o = send_core(parts_o)
    grad_next, parts_o = lax.optimization_barrier((grad_low, parts_o))
    out = (r1 + dot(act, w_o, 1, 1) + biases[1]).astype(BF)
    block_out = dot(after(out), turn, 1, 1).astype(BF)

    grad = grad_low.astype(F32)
    d_bias_two = jnp.sum(grad, axis=0)
    du = (dot(grad_next, w_o, 1, 0) * slope).astype(BF)
    d_bias_f = jnp.sum(du.astype(F32), axis=0)
    du, came_o = lax.optimization_barrier((du, came_o))
    blocks_o = send(to_y_blocks(parts_o, came_o), "y")
    parts_f = [halves(a2, du)]
    came_f = send_core(parts_f)
    du, parts_f = lax.optimization_barrier((du, parts_f))
    da2 = after(dot(du, w_f, 1, 1))
    dv2, d_gain_two, d_shift_two = norm_back(da2, xhat2, inv2, gains[1])
    dr1 = grad + dv2
    g1 = dr1.astype(BF)
    d_bias_one = jnp.sum(g1.astype(F32), axis=0)
    parts_p = [halves(g1, attn)]
    came_p = send_core(parts_p)
    dattn = dot(g1, w_p, 1, 0).astype(BF)
    dattn, blocks_o, came_f, came_p = lax.optimization_barrier((dattn, blocks_o, came_f, came_p))
    blocks_f = to_y_blocks(parts_f + parts_p, came_f + came_p)
    dattn, blocks_f = lax.optimization_barrier((dattn, blocks_f))
    blocks_f = send(blocks_f, "y")
    filled = attend_back(qkv, probs, dattn, attn, 0)
    dq, dk, dv = attend_back(qkv, probs, dattn, attn, 3, tuple(filled))
    dq, dk, dv, blocks_f = together(dq, dk, dv, blocks_f)
    da1_prev = (dot(dk[:HALF], w_k, 1, 1) + dot(dv[:HALF], w_v, 1, 1)).astype(BF)
    blocks_u = y_then_z_blocks([blocks_o, blocks_f], [(1536,), (1536, 384)])
    da1_prev, blocks_u, dq, dk, dv = together(da1_prev, blocks_u, dq, dk, dv)
    da1_sent = lax.ppermute(da1_prev, "zl", [(1, 0)])
    blocks_u = send(blocks_u, Z)
    sent = [dot(u[:, 384:], v, 0, 0).astype(BF) for u, v in ((a1[HALF:], dq), (a1, dk), (a1, dv))]
    dq, dk, dv, sent = together(dq, dk, dv, sent)
    came = [swap(v, "core", 1) for v in sent]
    parts = [
        (dot(u[:, :384], v, 0, 0).astype(BF), None) for u, v in ((a1[HALF:], dq), (a1, dk), (a1, dv))
    ]
    parts, came = together(parts, came)
    blocks = to_y_blocks(parts, came)
    dq, dk, dv, blocks = together(dq, dk, dv, blocks)
    blocks = send(blocks, "y")
    da1 = dot(dq, w_q, 1, 1) + dot(dk[HALF:], w_k, 1, 1) + dot(dv[HALF:], w_v, 1, 1)
    da1, da1_sent = together(da1, da1_sent)
    da1 = da1 + da1_sent.astype(F32)
    dv1, d_gain_one, d_shift_one = norm_back(da1, xhat1, inv1, gains[0])
    d_tokens = dot(after((dr1 + dv1).astype(BF)), turn, 1, 1).astype(BF)

    d_bias_q = jnp.sum(dq.astype(F32), axis=0).reshape(2, 6, 64)
    d_bias_v = jnp.sum(dv.astype(F32), axis=0).reshape(2, 6, 64)
    d_bias_f = d_bias_f.reshape(2, 24, 64)
    per_head = jnp.concatenate([d_bias_q, d_bias_v, d_bias_f], 1)
    per_head = jnp.where(first_half, per_head, per_head[::-1]).reshape(72, 64).astype(BF)
    per_head = (dot(of_owner, per_head, 1, 1) * of_row).astype(BF)
    per_feature = jnp.stack(
        [d_gain_one, d_gain_two, d_shift_one, d_shift_two, d_bias_one, d_bias_two]
    ).astype(BF)
    extra = dot(per_feature, jnp.eye(6, 128, dtype=BF), 0, 0)
    extra = (extra + dot(per_head, (column == 6).astype(BF), 1, 0)).astype(BF)
    came = swap(extra[384:], "core", 1)
    extra = to_y_blocks([(extra[:384], None)], [came])
    blocks, extra = together(blocks, extra)
    extra = send(extra, "y")
    blocks = send(y_then_z_blocks([blocks, extra], [(384, 384, 384), ((128,))]), Z)
    sums = finish_x(total_of([blocks, blocks_u]))
    sum_one, sum_o, sum_f = sums[:, :1280], sums[:, 1280:2816], sums[:, 2816:]

    small = sum_one[:, 1152:]
    features = small[:, :6].reshape(2, 6, 6)
    features = jnp.where(first_half, features[0], features[1]).T
    heads = small[:, 6:12].T.reshape(2, 36)
    heads = jnp.where(first_half, heads[0], heads[1])
    return (
        block_out[None],
        d_tokens[None],
        jnp.stack([sum_one[:, :384], sum_one[:, 384:768], sum_one[:, 768:1152]]),
        heads[:12].reshape(2, 6, 1),
        sum_f[:, 1536:].T,
        sum_f[:, :1536],
        heads[12:].reshape(24, 1),
        sum_o.T,
        features[0:2],
        features[2:4],
        features[4:6],
    )


def solution(mesh):
    fine = Mesh(mesh.devices.reshape(2, 4, 4, 2, 2), AXES)
    both = P(None, DP + ("zl",))
    weights = (P(None, DP, "zl"), P(None, "zl", DP), P("zl", DP), P(DP, "zl"), P("zl", DP), P("zl", DP))
    wide = P(DP, "zl", None)
    return jax.shard_map(
        body,
        mesh=fine,
        in_specs=(wide, P(DP, "zl"), wide) + weights + (both, both, both),
        out_specs=(wide, wide) + weights + (both, both, both),
        check_vma=False,
    )
```

```python
import jax
import jax.numpy as jnp
from jax import lax
from jax.experimental import pallas as pl
from jax.experimental.pallas import tpu as pltpu
from jax.sharding import Mesh, PartitionSpec as P

AXES = ("zh", "y", "x", "core", "zl")
DP = ("zh", "y", "x", "core")
Z = ("zh", "zl")
HALF = 512
WIDTH = 768
FF = 3072
BF = jnp.bfloat16
F32 = jnp.float32
VMEM = 60 * 1024 * 1024


def swap(value, axis, bit):
    count = 2 if axis == "core" else 4
    return lax.ppermute(value, axis, [(i, i ^ bit) for i in range(count)])


def dot(a, b, ca, cb):
    return lax.dot_general(a, b, (((ca,), (cb,)), ((), ())), preferred_element_type=F32)


def together(*values):
    return lax.optimization_barrier(values)


def after(value, *earlier):
    return lax.optimization_barrier((value, earlier))[0]


def combine(inputs, outputs, plan):
    def kernel(*refs):
        sources, results = refs[: len(inputs)], refs[len(inputs) :]
        for out, r, c, rows, cols, terms in plan:
            read = [sources[i][a : a + rows, b : b + cols] for i, a, b in terms]
            total = read[0]
            if len(read) > 1:
                total = total.astype(F32)
                for term in read[1:]:
                    total = total + term.astype(F32)
            results[out][r : r + rows, c : c + cols] = total.astype(results[out].dtype)

    moved = sum(2 * v.size for v in inputs) + sum(2 * r * c for r, c in outputs)
    return pl.pallas_call(
        kernel,
        out_shape=[jax.ShapeDtypeStruct(shape, BF) for shape in outputs],
        compiler_params=pltpu.CompilerParams(vmem_limit_bytes=VMEM),
        cost_estimate=pl.CostEstimate(flops=0, bytes_accessed=moved, transcendentals=0),
    )(*inputs)


def place(inputs, outputs, plan):
    def kernel(*refs):
        sources = refs[: len(inputs)]
        results = refs[len(inputs) : len(inputs) + len(outputs)]
        sems = refs[-1]
        copies = [
            pltpu.make_async_copy(
                sources[i].at[a : a + rows, b : b + cols],
                results[out].at[r : r + rows, c : c + cols],
                sems.at[n],
            )
            for n, (out, r, c, rows, cols, (i, a, b)) in enumerate(plan)
        ]
        for copy in copies:
            copy.start()
        for copy in copies:
            copy.wait()

    return pl.pallas_call(
        kernel,
        out_shape=[jax.ShapeDtypeStruct(shape, BF) for shape in outputs],
        in_specs=[pl.BlockSpec(memory_space=pl.ANY)] * len(inputs),
        scratch_shapes=[pltpu.SemaphoreType.DMA((len(plan),))],
        compiler_params=pltpu.CompilerParams(vmem_limit_bytes=VMEM),
        cost_estimate=pl.CostEstimate(
            flops=0, bytes_accessed=sum(4 * r * c for r, c in outputs), transcendentals=0
        ),
    )(*inputs)


def others(part, axis):
    return [swap(part, axis, k) for k in (1, 2, 3)]


def join_z(pieces, widths):
    plan, at = [], 0
    for width in widths:
        for bit in range(4):
            plan.append((0, bit // 2 * 48, 2 * at + bit % 2 * width, 48, width, (bit, 0, at)))
        at += width
    return place(pieces, [(96, 2 * at)], plan)[0]


def join_y(pieces):
    width = pieces[0].shape[1]
    return place(pieces, [(192, width)], [(0, 48 * k, 0, 48, width, (k, 0, 0)) for k in range(4)])[0]


def with_core(pieces):
    return [swap(piece, "core", 1) for piece in pieces]


def around_first(part, axis):
    return swap(part, axis, 1), swap(part, axis, 3)


def assemble_y(pieces, cuts):
    plan, pairs = [], list(zip((0,) + cuts[:-1], cuts))
    for out, (a, b) in enumerate(pairs):
        row = 0
        for i, piece in enumerate(pieces):
            plan.append((out, row, 0, piece.shape[0], b - a, (i, 0, a)))
            row += piece.shape[0]
    return place(pieces, [(WIDTH, b - a) for a, b in pairs], plan)


def assemble_z(pieces):
    width = pieces[0].shape[1]
    plan = []
    for i in range(8):
        core, bit = i // 4, i % 4
        for k in range(4):
            row = core * 384 + k * 96 + bit // 2 * 48
            plan.append((0, row, bit % 2 * width, 48, width, (i, 48 * k, 0)))
    return place(pieces, [(WIDTH, 2 * width)], plan)[0]


def send_core(parts):
    return [swap(sent, "core", 1) for _, sent in parts]


def to_y_blocks(parts, came):
    plan, at, count = [], 0, len(parts)
    for i, (own, _) in enumerate(parts):
        width = own.shape[1]
        for k in range(4):
            plan.append((k, 0, at, 96, width, [(i, 96 * k, 0), (count + i, 96 * k, 0)]))
        at += width
    return combine([own for own, _ in parts] + came, [(96, at)] * 4, plan)


def to_z_blocks(parts, came):
    plan, at, count = [], 0, len(parts)
    for i, (own, _) in enumerate(parts):
        width = own.shape[1] // 2
        for bit in range(4):
            for k in range(4):
                row, col = 96 * k + bit // 2 * 48, bit % 2 * width
                plan.append((bit, 48 * k, at, 48, width, [(i, row, col), (count + i, row, col)]))
        at += width
    return combine([own for own, _ in parts] + came, [(192, at)] * 4, plan)


def send(blocks, axis):
    return [blocks[0]] + [swap(blocks[k], axis, k) for k in (1, 2, 3)]


def y_then_z_blocks(groups, widths):
    plan, at = [], 0
    for g, group_widths in enumerate(widths):
        col = 0
        for width in group_widths:
            for bit in range(4):
                shared = groups[g][0].shape[1] == width
                row, c = bit // 2 * 48, col + (0 if shared else bit % 2 * width)
                plan.append((bit, 0, at, 48, width, [(4 * g + i, row, c) for i in range(4)]))
            col += 2 * width
            at += width
    return combine(sum(groups, []), [(48, at)] * 4, plan)


def z_then_y_blocks(groups):
    plan, at = [], 0
    for g, group in enumerate(groups):
        width = group[0].shape[1]
        for k in range(4):
            plan.append((k, 0, at, 48, width, [(4 * g + i, 48 * k, 0) for i in range(4)]))
        at += width
    return combine(sum(groups, []), [(48, at)] * 4, plan)


def total_of(groups):
    plan, at = [], 0
    for g, group in enumerate(groups):
        width = group[0].shape[1]
        plan.append((0, 0, at, 48, width, [(4 * g + i, 0, 0) for i in range(4)]))
        at += width
    return combine(sum(groups, []), [(48, at)], plan)[0]


def finish_x(low):
    total = low[:12].astype(F32)
    for k in (1, 2, 3):
        total = total + swap(low[12 * k : 12 * k + 12], "x", k).astype(F32)
    return total


def halves(a, b):
    return dot(a[:, :384], b, 0, 0).astype(BF), dot(a[:, 384:], b, 0, 0).astype(BF)


def lanes_of(head, value):
    lane = lax.broadcasted_iota(jnp.int32, value.shape, 1)
    return jnp.where((lane >= 64) == (head == 1), value, jnp.zeros_like(value))


def attend_kernel(q_ref, k_ref, v_ref, segq_ref, segk_ref, out_ref, p_ref, bias_ref):
    @pl.when(pl.program_id(0) == 0)
    def _():
        place_k = lax.broadcasted_iota(jnp.int32, (2 * HALF, HALF), 0)
        place_q = lax.broadcasted_iota(jnp.int32, (2 * HALF, HALF), 1) + HALF
        allowed = (segk_ref[...] == segq_ref[...]) & (place_k <= place_q)
        bias_ref[...] = jnp.where(allowed, 0.0, -1e30)

    for block in range(2):
        keys = HALF + 256 * (block + 1)
        rows = slice(256 * block, 256 * (block + 1))
        q = q_ref[rows, :] * 0.125
        k = k_ref[:keys, :]
        mixed = []
        for head in range(2):
            s = dot(k, lanes_of(head, q), 1, 1) + bias_ref[:keys, rows]
            e = jnp.exp(s - jnp.max(s, axis=0, keepdims=True))
            p = (e * (1.0 / jnp.sum(e, axis=0, keepdims=True))).astype(BF)
            p_ref[head, :keys, rows] = p
            mixed.append(dot(v_ref[:keys, :], p, 0, 0))
        feature = lax.broadcasted_iota(jnp.int32, mixed[0].shape, 0)
        out_ref[rows, :] = jnp.where(feature < 64, mixed[0], mixed[1]).T.astype(BF)


def attend(qkv, seg_q, seg_k):
    whole = lambda shape: pl.BlockSpec(shape, lambda i: (0, 0))
    return pl.pallas_call(
        attend_kernel,
        grid=(6,),
        in_specs=[
            pl.BlockSpec((HALF, 128), lambda i: (1, i)),
            pl.BlockSpec((2 * HALF, 128), lambda i: (0, i + 6)),
            pl.BlockSpec((2 * HALF, 128), lambda i: (0, i + 12)),
            whole((1, HALF)),
            whole((2 * HALF, 1)),
        ],
        out_specs=[
            pl.BlockSpec((HALF, 128), lambda i: (0, i)),
            pl.BlockSpec((2, 2 * HALF, HALF), lambda i: (i, 0, 0)),
        ],
        out_shape=[
            jax.ShapeDtypeStruct((HALF, WIDTH), BF),
            jax.ShapeDtypeStruct((12, 2 * HALF, HALF), BF),
        ],
        scratch_shapes=[pltpu.VMEM((2 * HALF, HALF), F32)],
        compiler_params=pltpu.CompilerParams(vmem_limit_bytes=VMEM),
        cost_estimate=pl.CostEstimate(
            flops=12 * HALF * HALF * 2 * 64 * 4, bytes_accessed=18_000_000, transcendentals=6_000_000
        ),
    )(qkv, qkv, qkv, seg_q, seg_k)


def attend_back_kernel(q_ref, k_ref, v_ref, p_ref, g_ref, attn_ref, dq_ref, dk_ref, dv_ref, sq_ref, sv_ref):
    dk_sum, dv_sum = None, None
    added = lambda v: jnp.sum(v.astype(F32), axis=0, keepdims=True)
    for block in range(2):
        keys = HALF + 256 * (block + 1)
        rows = slice(256 * block, 256 * (block + 1))
        q = q_ref[rows, :] * 0.125
        g = g_ref[rows, :]
        through = (g.astype(F32) * attn_ref[rows, :].astype(F32)).T
        k = k_ref[:keys, :]
        v = v_ref[:keys, :]
        dq, dk, dv = [], [], []
        for head in range(2):
            p = p_ref[head, :keys, rows]
            dp = dot(v, lanes_of(head, g), 1, 1)
            wide = p.astype(F32)
            inner = jnp.sum(through[64 * head : 64 * head + 64], axis=0, keepdims=True)
            ds = (wide * (dp - inner)).astype(BF)
            dv.append(dot(p, g, 1, 0))
            dk.append(dot(ds, q, 1, 0))
            dq.append(dot(k, ds, 0, 0))
        feature = lax.broadcasted_iota(jnp.int32, dq[0].shape, 0)
        low = (jnp.where(feature < 64, dq[0], dq[1]).T * 0.125).astype(BF)
        dq_ref[rows, :] = low
        sq_ref[...] = added(low) if block == 0 else sq_ref[...] + added(low)
        lane = lax.broadcasted_iota(jnp.int32, dk[0].shape, 1)
        dk = jnp.where(lane < 64, dk[0], dk[1])
        dv = jnp.where(lane < 64, dv[0], dv[1])
        if block == 0:
            dk_sum, dv_sum = dk, dv
        else:
            seen = HALF + 256
            dk_ref[:seen, :] = (dk_sum + dk[:seen]).astype(BF)
            early, late = (dv_sum + dv[:seen]).astype(BF), dv[seen:].astype(BF)
            dv_ref[:seen, :] = early
            dk_ref[seen:, :] = dk[seen:].astype(BF)
            dv_ref[seen:, :] = late
            sv_ref[...] = added(early) + added(late)


def attend_back(qkv, p, grad, attn):
    narrow = pl.BlockSpec((HALF, 128), lambda i: (0, i))
    tall = pl.BlockSpec((2 * HALF, 128), lambda i: (0, i))
    line = pl.BlockSpec((1, 128), lambda i: (0, i))
    return pl.pallas_call(
        attend_back_kernel,
        grid=(6,),
        in_specs=[
            pl.BlockSpec((HALF, 128), lambda i: (1, i)),
            pl.BlockSpec((2 * HALF, 128), lambda i: (0, i + 6)),
            pl.BlockSpec((2 * HALF, 128), lambda i: (0, i + 12)),
            pl.BlockSpec((2, 2 * HALF, HALF), lambda i: (i, 0, 0)),
            narrow,
            narrow,
        ],
        out_specs=[narrow, tall, tall, line, line],
        out_shape=[
            jax.ShapeDtypeStruct((HALF, WIDTH), BF),
            jax.ShapeDtypeStruct((2 * HALF, WIDTH), BF),
            jax.ShapeDtypeStruct((2 * HALF, WIDTH), BF),
            jax.ShapeDtypeStruct((1, WIDTH), F32),
            jax.ShapeDtypeStruct((1, WIDTH), F32),
        ],
        compiler_params=pltpu.CompilerParams(vmem_limit_bytes=VMEM),
        cost_estimate=pl.CostEstimate(
            flops=12 * HALF * HALF * 2 * 64 * 8, bytes_accessed=20_000_000, transcendentals=0
        ),
    )(qkv, qkv, qkv, p, grad, attn)


def standard(values):
    centred = values - jnp.mean(values, axis=-1, keepdims=True)
    variance = jnp.mean(centred * centred, axis=-1, keepdims=True)
    inverse = lax.rsqrt(variance + 1e-05)
    return centred * inverse, inverse


def norm_back(gradient, normed, inverse, gain):
    scaled = gradient * gain
    first = jnp.mean(scaled, axis=-1, keepdims=True)
    second = jnp.mean(scaled * normed, axis=-1, keepdims=True)
    return (
        inverse * (scaled - first - normed * second),
        jnp.sum(gradient * normed, axis=0),
        jnp.sum(gradient, axis=0),
    )


def gelu_both(u):
    inner = 0.7978845608028654 * (u + 0.044715 * u * u * u)
    t = jnp.tanh(inner)
    slope = 0.7978845608028654 * (1.0 + 3.0 * 0.044715 * u * u)
    return 0.5 * u * (1.0 + t), 0.5 * (1.0 + t) + 0.5 * u * (1.0 - t * t) * slope


def feature_order():
    place = jnp.arange(WIDTH, dtype=jnp.int32)
    row, owner = place % 12, place // 12
    zh = lax.axis_index("zh") ^ (owner // 4 % 2)
    y = lax.axis_index("y") ^ (owner // 8 % 4)
    x = lax.axis_index("x") ^ (owner % 4)
    core = lax.axis_index("core") ^ (owner // 32)
    return ((zh * 4 + y) * 4 + x) * 2 + core, row


def body(
    tokens, segments, cotangent, w_qkv, b_qv, w_proj, w_fc, b_fc, w_out, ln_gains, ln_biases, out_biases
):
    first_half = lax.axis_index("zl") == 0
    before = lambda v: lax.ppermute(v, "zl", [(0, 1)])
    vectors = jnp.concatenate([ln_gains, ln_biases, out_biases], 0)
    high = lax.reduce_precision(vectors, 8, 7)
    middle = lax.reduce_precision(vectors - high, 8, 7)
    terms = jnp.concatenate([high, middle, vectors - high - middle], 0).T
    empty = jnp.zeros_like(terms)
    terms = jnp.where(
        first_half, jnp.concatenate([terms, empty], 0), jnp.concatenate([empty, terms], 0)
    ).astype(BF)
    extra = jnp.concatenate(
        [terms, b_qv.reshape(12, 1), b_fc.reshape(2, 12).T, jnp.zeros((12, 107), BF)], 1
    )
    weights = jnp.concatenate([*w_qkv, extra, w_fc, w_out.T, w_proj.T], 1)
    pieces, prev_a, prev_segments = together(
        [weights] + others(weights, "x"), before(tokens[0, :256]), before(segments[0])
    )
    prev_segments = jnp.where(first_half, -1, prev_segments)
    one, two, three = [
        jnp.concatenate([v[:, a:b] for v in pieces], 0)
        for a, b in ((0, 1280), (1280, 2816), (2816, 4736))
    ]
    one = join_z([one] + others(one, Z), (384, 384, 384, 128))
    late, cot = after((tokens[0, 256:], cotangent[0]), one)

    owner, row = feature_order()
    turn = (
        jnp.arange(WIDTH, dtype=jnp.int32)[:, None] == (owner * 12 + row)[None, :]
    ).astype(BF)
    index = lambda n: jnp.arange(n, dtype=jnp.int32)
    of_owner = (owner[:, None] == index(64)[None, :]).astype(BF)
    of_row = (row[:, None] == index(72)[None, :] % 12).astype(F32)
    column = (index(128)[None, :] - index(72)[:, None] // 12).astype(F32)
    turn, of_owner, of_row, column = together(turn, of_owner, of_row, column)

    prev_b = before(late)
    three = after(three, prev_b)
    own_core, prev_b, pieces, ones = together(
        with_core([one]), prev_b, [three] + others(three, Z), others(one, "y")
    )
    three = join_z(pieces, (1536, 384))
    whole_row = jnp.concatenate([prev_a, prev_b, tokens[0]], 0)
    stream = dot(whole_row, turn, 1, 0).astype(BF).astype(F32)
    grad_low = dot(cot, turn, 1, 0).astype(BF)
    xhat1, inv1 = standard(stream)
    ones_core, xhat1, inv1, grad_low = together(with_core(ones), xhat1, inv1, grad_low)
    two = after(two, ones_core)
    pieces = [two] + others(two, "y")
    one, small = assemble_y([one] + ones + own_core + ones_core, (2304, 2560))
    w_q, w_k, w_v = one[:, :768], one[:, 768:1536], one[:, 1536:]

    terms = ((index(128)[None, :] % 6 == index(8)[:, None]) & (index(128)[None, :] < 18)).astype(BF)
    vectors = dot(terms, small[:, :128], 1, 1) + dot(terms, small[:, 128:], 1, 1)
    gains, shifts, biases = vectors[0:2], vectors[2:4], vectors[4:6]

    def entries(part):
        spread = dot(part, (column[:36] == 18).astype(BF), 1, 1) * of_row[:, :36]
        return dot(spread.astype(BF), of_owner, 0, 0)

    own_bias, other_bias = entries(small[:, :128]), entries(small[:, 128:])
    rows_of = lambda a, b: jnp.concatenate([own_bias[a:b], other_bias[a:b]], 0).reshape(-1)
    bias_q, bias_v, bias_f = rows_of(0, 6), rows_of(6, 12), rows_of(12, 36)

    a1 = (xhat1 * gains[0] + shifts[0]).astype(BF)
    a1, pieces, three = together(a1, pieces, three)
    two = join_y(pieces)
    two, three, a1 = together(two, three, a1)
    two_round, three_round = around_first(two, Z), around_first(three, "y")
    stream, xhat1, inv1 = stream[HALF:], xhat1[HALF:], inv1[HALF:]
    zeros = jnp.zeros((WIDTH,), F32)
    qkv_bias = jnp.concatenate([bias_q, zeros, bias_v])
    qkv = (dot(a1, one, 1, 0) + qkv_bias).astype(BF)
    seg_k = jnp.concatenate([prev_segments, segments[0]], 0)[:, None]
    qkv, two, three, two_round, three_round = together(qkv, two, three, two_round, three_round)
    two_far, three_far = swap(two, Z, 2), swap(three, "y", 2)
    two_core, three_core = with_core([two]), with_core([three])
    attn, probs = attend(qkv, segments, seg_k)
    attn, two_far, three_far, two_core, three_core, two_round, three_round = together(
        attn, two_far, three_far, two_core, three_core, two_round, three_round
    )
    two_rest = [two_round[0], two_far, two_round[1]]
    three_rest = [three_round[0], three_far, three_round[1]]
    two = [two] + two_rest + two_core + with_core(two_rest)
    three = [three] + three_rest + three_core + with_core(three_rest)
    w_o, w_p = assemble_y(three, (3072, 3840))
    w_f = assemble_z(two)

    r1 = stream + dot(attn, w_p, 1, 1) + biases[0]
    xhat2, inv2 = standard(r1)
    a2 = (xhat2 * gains[1] + shifts[1]).astype(BF)
    act, slope = gelu_both(dot(a2, w_f, 1, 0) + bias_f)
    act = act.astype(BF)
    parts_o = [halves(grad_low, act)]
    came_o = send_core(parts_o)
    grad_next, parts_o = lax.optimization_barrier((grad_low, parts_o))
    out = (r1 + dot(act, w_o, 1, 1) + biases[1]).astype(BF)
    block_out = dot(after(out), turn, 1, 1).astype(BF)

    grad = grad_low.astype(F32)
    d_bias_two = jnp.sum(grad, axis=0)
    du = (dot(grad_next, w_o, 1, 0) * slope).astype(BF)
    d_bias_f = jnp.sum(du.astype(F32), axis=0)
    du, came_o = lax.optimization_barrier((du, came_o))
    blocks_o = send(to_y_blocks(parts_o, came_o), "y")
    parts_f = [halves(a2, du)]
    came_f = send_core(parts_f)
    du, parts_f = lax.optimization_barrier((du, parts_f))
    da2 = after(dot(du, w_f, 1, 1))
    dv2, d_gain_two, d_shift_two = norm_back(da2, xhat2, inv2, gains[1])
    dr1 = grad + dv2
    g1 = dr1.astype(BF)
    d_bias_one = jnp.sum(g1.astype(F32), axis=0)
    parts_p = [halves(g1, attn)]
    came_p = send_core(parts_p)
    dattn = dot(g1, w_p, 1, 0).astype(BF)
    dattn, blocks_o, came_f, came_p = lax.optimization_barrier((dattn, blocks_o, came_f, came_p))
    blocks_f = to_y_blocks(parts_f + parts_p, came_f + came_p)
    dattn, blocks_f = lax.optimization_barrier((dattn, blocks_f))
    blocks_f = send(blocks_f, "y")
    dq, dk, dv, sum_q, sum_v = attend_back(qkv, probs, dattn, attn)
    dq, dk, dv, blocks_f = together(dq, dk, dv, blocks_f)
    da1_prev = (dot(dk[:HALF], w_k, 1, 1) + dot(dv[:HALF], w_v, 1, 1)).astype(BF)
    blocks_u = y_then_z_blocks([blocks_o, blocks_f], [(1536,), (1536, 384)])
    da1_prev, blocks_u, dq, dk, dv = together(da1_prev, blocks_u, dq, dk, dv)
    da1_sent = lax.ppermute(da1_prev, "zl", [(1, 0)])
    blocks_u = send(blocks_u, Z)
    sent = [dot(u[:, 384:], v, 0, 0).astype(BF) for u, v in ((a1[HALF:], dq), (a1, dk), (a1, dv))]
    dq, dk, dv, sent = together(dq, dk, dv, sent)
    came = [swap(v, "core", 1) for v in sent]
    parts = [
        (dot(u[:, :384], v, 0, 0).astype(BF), None) for u, v in ((a1[HALF:], dq), (a1, dk), (a1, dv))
    ]
    parts, came = together(parts, came)
    blocks = to_y_blocks(parts, came)
    dq, dk, dv, blocks = together(dq, dk, dv, blocks)
    blocks = send(blocks, "y")
    da1 = dot(dq, w_q, 1, 1) + dot(dk[HALF:], w_k, 1, 1) + dot(dv[HALF:], w_v, 1, 1)
    da1, da1_sent = together(da1, da1_sent)
    da1 = da1 + da1_sent.astype(F32)
    dv1, d_gain_one, d_shift_one = norm_back(da1, xhat1, inv1, gains[0])
    d_tokens = dot(after((dr1 + dv1).astype(BF)), turn, 1, 1).astype(BF)

    d_bias_q = sum_q.reshape(2, 6, 64)
    d_bias_v = sum_v.reshape(2, 6, 64)
    d_bias_f = d_bias_f.reshape(2, 24, 64)
    per_head = jnp.concatenate([d_bias_q, d_bias_v, d_bias_f], 1)
    per_head = jnp.where(first_half, per_head, per_head[::-1]).reshape(72, 64).astype(BF)
    per_head = (dot(of_owner, per_head, 1, 1) * of_row).astype(BF)
    per_feature = jnp.stack(
        [d_gain_one, d_gain_two, d_shift_one, d_shift_two, d_bias_one, d_bias_two]
    ).astype(BF)
    extra = dot(per_feature, jnp.eye(6, 128, dtype=BF), 0, 0)
    extra = (extra + dot(per_head, (column == 6).astype(BF), 1, 0)).astype(BF)
    came = swap(extra[384:], "core", 1)
    extra = to_y_blocks([(extra[:384], None)], [came])
    blocks, extra = together(blocks, extra)
    extra = send(extra, "y")
    blocks = send(y_then_z_blocks([blocks, extra], [(384, 384, 384), ((128,))]), Z)
    sums = finish_x(total_of([blocks, blocks_u]))
    sum_one, sum_o, sum_f = sums[:, :1280], sums[:, 1280:2816], sums[:, 2816:]

    small = sum_one[:, 1152:]
    features = small[:, :6].reshape(2, 6, 6)
    features = jnp.where(first_half, features[0], features[1]).T
    heads = small[:, 6:12].T.reshape(2, 36)
    heads = jnp.where(first_half, heads[0], heads[1])
    return (
        block_out[None],
        d_tokens[None],
        jnp.stack([sum_one[:, :384], sum_one[:, 384:768], sum_one[:, 768:1152]]),
        heads[:12].reshape(2, 6, 1),
        sum_f[:, 1536:].T,
        sum_f[:, :1536],
        heads[12:].reshape(24, 1),
        sum_o.T,
        features[0:2],
        features[2:4],
        features[4:6],
    )


def solution(mesh):
    fine = Mesh(mesh.devices.reshape(2, 4, 4, 2, 2), AXES)
    both = P(None, DP + ("zl",))
    weights = (P(None, DP, "zl"), P(None, "zl", DP), P("zl", DP), P(DP, "zl"), P("zl", DP), P("zl", DP))
    wide = P(DP, "zl", None)
    return jax.shard_map(
        body,
        mesh=fine,
        in_specs=(wide, P(DP, "zl"), wide) + weights + (both, both, both),
        out_specs=(wide, wide) + weights + (both, both, both),
        check_vma=False,
    )
```
